32 devices in a mesh: pipe: 8 (over z, core), dp: 4 (over y, x).
Axes of the slice: x: 2, y: 2, z: 4, core: 2. Of those that a mesh axis runs over, the one named last changes fastest.
Arguments:
- stash_held: bfloat16 [8, 512, 4096], P('pipe', 'dp'), may hold values from -36 to 36
- grad_in: bfloat16 [8, 512, 4096], P('pipe', 'dp'), may hold values from -6 to 6
- w_down: bfloat16 [8, 4096, 128], P('pipe'), may hold values from -0.09375 to 0.09375
- w_up: bfloat16 [8, 128, 4096], P('pipe'), may hold values from -0.5 to 0.5
- gain: float32 [8, 4096], P('pipe'), may hold values from 0.1 to 1.9
Outputs:
- prev_grad: bfloat16 [8, 512, 4096], P('pipe', 'dp')
- grad_down: float32 [8, 4096, 128], P('pipe', 'dp')
- grad_up: float32 [8, 128, 4096], P('pipe', None, 'dp')
The draws below stay inside these ranges and needn't reach their ends.
All inputs are finite; a program needn't handle non-finite values.
Results may differ from the reference program's by a relative error of at most 0.0055.
Values may be sent and summed in bfloat16 or wider, within the bound.
No kernel may reach another device: no remote copies, remote signals or barrier semaphores. Data moves between devices by JAX's collectives and lax.ppermute only.
A program may use at most 64 MiB of HBM per device.

```python
import math
import jax
import jax.numpy as jnp
from jax import lax

D = 4096
RANK = 128
SECTIONS = 8
TOKENS = 512


def draw_stash_held(key, part):
    key = jax.random.fold_in(key, 11)
    first, second, third = jax.random.split(key, 3)
    shape = (SECTIONS, TOKENS, D)
    base = jnp.clip(jax.random.normal(first, shape, jnp.float32), -4.0, 4.0)
    lower, upper = (0.3, 3.0)
    row_scale = jnp.exp(jax.random.uniform(second, (SECTIONS, TOKENS, 1), jnp.float32, math.log(lower), math.log(upper)))
    col_scale = jnp.exp(jax.random.uniform(third, (SECTIONS, 1, D), jnp.float32, math.log(lower), math.log(upper)))
    return (base * row_scale * col_scale).astype(jnp.bfloat16)


def with_spikes(result, key, source, target, parts, factor):
    owner, partner = [(jnp.arange(result.shape[dim]) // (result.shape[dim] // parts)).reshape([-1 if axis == dim else 1 for axis in range(result.ndim)]) for dim in (source, target)]
    chosen = jax.random.permutation(key, parts)[partner]
    strong = (owner == chosen) | (owner == (partner + parts // 2) % parts)
    return jnp.where(strong, factor * result, result)


def levels(rng, dims, cuts, low, largest):
    def one(position, shards_of):
        heights = jax.random.uniform(jax.random.fold_in(jax.random.fold_in(rng, 6), position), (shards_of,), jnp.float32, low / len(cuts), largest / len(cuts))
        return jnp.repeat(jnp.exp(heights), dims[position] // shards_of).reshape((-1,) + (1,) * (len(dims) - position - 1))

    level = one(*cuts[0])
    for cut in cuts[1:]:
        level = level * one(*cut)
    return level


def centred(key, shape, spread, bound, pieces=(), held_as=jnp.bfloat16):
    level = levels(key, shape, pieces, -0.22, 0.18) if pieces else 1.0
    drawn = jax.random.normal(key, shape, jnp.float32) * spread * level
    return jnp.minimum(jnp.maximum(drawn, -bound), bound).astype(held_as)


def noise_with(rng, extent, spread, limit, cuts, heavy, held_as=jnp.bfloat16):
    entries = spread * jax.random.normal(rng, extent, jnp.float32)
    if cuts:
        entries = entries * levels(rng, extent, cuts, -0.22, 0.18)
    return jnp.clip(with_spikes(entries, jax.random.fold_in(rng, 3), *heavy), -limit, limit).astype(held_as)


def setup_inputs(seed: int = 0) -> dict:
    key_list = jax.random.split(jax.random.key(seed), 6)
    stash_held = draw_stash_held(jax.random.fold_in(key_list[5], 71), 0)
    grad_in = noise_with(key_list[1], (SECTIONS, TOKENS, D), 1.0, 6.0, ((0, 8), (1, 4)), (1, 2, 4, 2.0))
    w_down = centred(key_list[2], (SECTIONS, D, RANK), D ** -0.5, 0.09375, ((0, 8),))
    w_up = centred(key_list[3], (SECTIONS, RANK, D), RANK ** -0.5, 0.5, ((0, 8),))
    gain = jnp.clip(1.0 + 0.18 * jax.random.normal(key_list[4], (SECTIONS, D), jnp.float32), 0.1, 1.9)
    return dict(stash_held=stash_held, grad_in=grad_in, w_down=w_down, w_up=w_up, gain=gain)


def section_backward(saved, cot, w_down, w_up, gain):
    xf = saved.astype(jnp.float32)
    rms = jnp.sqrt(lax.optimization_barrier(jnp.mean(xf * xf, axis=1, keepdims=True)) + 1e-05)
    unit = xf / rms
    normed = (unit * gain[None, :]).astype(jnp.bfloat16)
    pre = jnp.dot(normed, w_down, preferred_element_type=jnp.float32)
    act, pull = jax.vjp(lambda value: jax.nn.gelu(value, approximate=True), pre)
    act_b = act.astype(jnp.bfloat16)
    dact = jnp.dot(cot, w_up.T, preferred_element_type=jnp.float32)
    dpre = pull(dact)[0].astype(jnp.bfloat16)
    up_grad = jnp.dot(act_b.T, cot, preferred_element_type=jnp.float32)
    down_grad = jnp.dot(normed.T, dpre, preferred_element_type=jnp.float32)
    dnorm = jnp.dot(dpre, w_down.T, preferred_element_type=jnp.float32) * gain[None, :]
    inner = lax.optimization_barrier(jnp.mean(dnorm * unit, axis=1, keepdims=True))
    dx = cot.astype(jnp.float32) + (dnorm - unit * inner) / rms
    return (dx.astype(jnp.bfloat16), down_grad, up_grad)

def reference(stash_held, grad_in, w_down, w_up, gain):
    saved = jnp.roll(stash_held, -(SECTIONS // 2), axis=0)

    def one_section(items):
        return section_backward(items[0], items[1], items[2], items[3], items[4])
    dx, down_grad, up_grad = lax.map(one_section, (saved, grad_in, w_down, w_up, gain))
    prev_grad = jnp.concatenate([dx[1:], jnp.zeros_like(dx[:1])], axis=0)
    return (prev_grad, down_grad, up_grad)
```

```python
import jax
import jax.numpy as jnp
from jax import lax
from jax.sharding import PartitionSpec as P

CHUNKS = 4


def exchanged(x, axis, mask):
    return lax.ppermute(x, axis, [(i, i ^ mask) for i in range(lax.axis_size(axis))])


def to_previous(x, axis):
    return lax.ppermute(x, axis, [(i, i - 1) for i in range(1, lax.axis_size(axis))])


def rows_dot(a, b):
    return lax.dot_general(a, b, (((0,), (0,)), ((), ())), preferred_element_type=jnp.float32)


def last_dot(a, b):
    return lax.dot_general(a, b, (((1,), (1,)), ((), ())), preferred_element_type=jnp.float32)


def per_device(stash_held, grad_in, w_down, w_up, gain):
    sections = lax.axis_size("pipe")
    groups = lax.axis_size("dp")
    me = lax.axis_index("dp")
    stash, cot, down, upper, scale = stash_held[0], grad_in[0], w_down[0], w_up[0], gain
    tokens, features = cot.shape
    rank = down.shape[1]
    rows = tokens // CHUNKS
    width = features // groups

    def block(x, k):
        return lax.dynamic_slice_in_dim(x, (me ^ k) * width, width, axis=1)

    parts = [slice(i * rows, (i + 1) * rows) for i in range(CHUNKS)]
    arrivals = [exchanged(stash[part], "pipe", sections // 2) for part in parts]
    cot_all = [block(cot, 0)] + [exchanged(block(cot, k), "dp", k) for k in range(1, groups)]
    dact = last_dot(cot, upper)

    before = []
    packs = []
    for part, saved in zip(parts, arrivals):
        xf = saved.astype(jnp.float32)
        rms = jnp.sqrt(jnp.mean(xf * xf, axis=1, keepdims=True) + 1e-05)
        unit = xf / rms
        normed = (unit * scale).astype(jnp.bfloat16)
        pre = jnp.dot(normed, down, preferred_element_type=jnp.float32)
        act, pull = jax.vjp(lambda value: jax.nn.gelu(value, approximate=True), pre)
        act = act.astype(jnp.bfloat16)
        dpre = pull(dact[part])[0].astype(jnp.bfloat16)
        inner = jnp.sum(dpre.astype(jnp.float32) * pre, axis=1, keepdims=True) / features
        dnorm = last_dot(dpre, down) * scale
        dx = (cot[part].astype(jnp.float32) + (dnorm - unit * inner) / rms).astype(jnp.bfloat16)
        before.append(to_previous(dx, "pipe"))
        pack = [jnp.concatenate([block(normed, k), dpre, act], axis=1) for k in range(groups)]
        packs.append([pack[0]] + [exchanged(pack[k], "dp", k) for k in range(1, groups)])

    every = jnp.concatenate([packs[i][k] for k in range(groups) for i in range(CHUNKS)], axis=0)
    normed_all = every[:, :width]
    dpre_all = every[:, width : width + rank]
    act_all = every[:, width + rank :]
    down_grad = rows_dot(normed_all, dpre_all)
    up_grad = rows_dot(act_all, jnp.concatenate(cot_all, axis=0))
    return (jnp.concatenate(before, axis=0)[None], down_grad[None], up_grad[None])


def solution(mesh):
    in_specs = (
        P("pipe", "dp", None),
        P("pipe", "dp", None),
        P("pipe", None, None),
        P("pipe", None, None),
        P("pipe", None),
    )
    out_specs = (P("pipe", "dp", None), P("pipe", "dp", None), P("pipe", None, "dp"))
    return jax.shard_map(
        per_device, mesh=mesh, in_specs=in_specs, out_specs=out_specs, check_vma=False
    )
```

```python
import functools
import math
import jax
import jax.numpy as jnp
from jax import lax
from jax.experimental import pallas as pl
from jax.experimental.pallas import tpu as pltpu
from jax.sharding import PartitionSpec as P

SHARES = (2, 2, 2, 2)
AHEAD = 2
LANES = 512
VMEM = pl.BlockSpec(memory_space=pltpu.VMEM)
SMEM = pl.BlockSpec(memory_space=pltpu.SMEM)
ANY = pl.BlockSpec(memory_space=pl.ANY)
PARAMS = pltpu.CompilerParams(vmem_limit_bytes=32 * 1024 * 1024)


def exchanged(x, axis, mask):
    return lax.ppermute(x, axis, [(i, i ^ mask) for i in range(lax.axis_size(axis))])


def to_previous(x, axis):
    return lax.ppermute(x, axis, [(i, i - 1) for i in range(1, lax.axis_size(axis))])


def rows_dot(a, b):
    return lax.dot_general(a, b, (((0,), (0,)), ((), ())), preferred_element_type=jnp.float32)


def last_dot(a, b):
    return lax.dot_general(a, b, (((1,), (1,)), ((), ())), preferred_element_type=jnp.float32)


def gelu_and_slope(x):
    c = math.sqrt(2.0 / math.pi)
    th = jnp.tanh(c * (x + 0.044715 * (x * x * x)))
    slope = 0.5 * (1.0 + th) + 0.5 * x * (1.0 - th * th) * (c * (1.0 + 3.0 * 0.044715 * (x * x)))
    return 0.5 * x * (1.0 + th), slope


def chunk_kernel(groups, start, following, waits, me_ref, saved_ref, cot_ref, dact_ref, down_ref, gain_ref, stash_ref, *refs):
    outs = refs[waits:]
    dx_ref, pack_refs = outs[0], outs[1 : 1 + groups]
    rest = outs[1 + groups :]
    normed_ref = rest[-2] if following else rest[-1]
    copy = None
    if following:
        copy = pltpu.make_async_copy(stash_ref.at[pl.ds(*following)], rest[0], rest[-1])
        copy.start()
    rows, features = saved_ref.shape
    width = features // groups
    rank = down_ref.shape[1]
    lanes = [pl.ds(f, LANES) for f in range(0, features, LANES)]
    total = jnp.zeros((rows, 1), jnp.float32)
    for at in lanes:
        xf = saved_ref[:, at].astype(jnp.float32)
        total += jnp.sum(xf * xf, axis=1, keepdims=True)
    inverse = 1.0 / jnp.sqrt(total / features + 1e-05)
    for at in lanes:
        unit = saved_ref[:, at].astype(jnp.float32) * inverse
        normed_ref[:, at] = (unit * gain_ref[:, at]).astype(jnp.bfloat16)
    pre = jnp.dot(normed_ref[...], down_ref[...], preferred_element_type=jnp.float32)
    act, slope = gelu_and_slope(pre)
    act = act.astype(jnp.bfloat16)
    dpre = (dact_ref[pl.ds(start, rows), :] * slope).astype(jnp.bfloat16)
    inner = jnp.sum(dpre.astype(jnp.float32) * pre, axis=1, keepdims=True) / features
    for k in range(groups):
        at = pl.ds(pl.multiple_of((me_ref[0] ^ k) * width, 128), width)
        pack_refs[k][:, :width] = normed_ref[:, at]
        pack_refs[k][:, width : width + rank] = dpre
        pack_refs[k][:, width + rank :] = act
    pull = inner * inverse
    for at in lanes:
        dnorm = last_dot(dpre, down_ref[at, :]) * gain_ref[:, at]
        xf = saved_ref[:, at].astype(jnp.float32)
        held = cot_ref[pl.ds(start, rows), at].astype(jnp.float32)
        dx_ref[:, at] = (held + (dnorm - xf * pull) * inverse).astype(jnp.bfloat16)
    if copy is not None:
        copy.wait()


def run_chunk(me, saved, cot, dact, down, gain, stash, start, following, waits, groups):
    rows, features = saved.shape
    rank = down.shape[1]
    pack = jax.ShapeDtypeStruct((rows, features // groups + 2 * rank), jnp.bfloat16)
    outs = [jax.ShapeDtypeStruct((rows, features), jnp.bfloat16)] + [pack] * groups
    specs = [VMEM] * len(outs)
    scratch = [pltpu.VMEM((rows, features), jnp.bfloat16)]
    if following:
        outs.append(jax.ShapeDtypeStruct((following[1], features), jnp.bfloat16))
        specs.append(ANY)
        scratch.append(pltpu.SemaphoreType.DMA)
    got = pl.pallas_call(
        functools.partial(chunk_kernel, groups, start, following, len(waits)),
        out_shape=outs,
        in_specs=[SMEM] + [VMEM] * 5 + [ANY] * (1 + len(waits)),
        out_specs=specs,
        scratch_shapes=scratch,
        compiler_params=PARAMS,
    )(me, saved, cot, dact, down, gain, stash, *waits)
    return got[0], got[1 : 1 + groups], got[1 + groups :]


def sum_kernel(groups, spans, first, *refs):
    count = groups * len(spans)
    packs, cots = refs[:count], refs[count : count + groups]
    rest = refs[count + groups :]
    olds, rest = ((), rest) if first else (rest[:2], rest[2:])
    down_ref, up_ref, every, held = rest
    width = held.shape[1]
    rank = up_ref.shape[0]
    at = 0
    for k in range(groups):
        for j, (start, rows) in enumerate(spans):
            every[pl.ds(at, rows), :] = packs[k * len(spans) + j][...]
            held[pl.ds(at, rows), :] = cots[k][pl.ds(start, rows), :]
            at += rows
    down = rows_dot(every[:, :width], every[:, width : width + rank])
    up = rows_dot(every[:, width + rank :], held[...])
    down_ref[...] = down if first else down + olds[0][...]
    up_ref[...] = up if first else up + olds[1][...]


def run_sum(packs, cots, spans, olds, rank):
    groups = len(cots)
    width = cots[0].shape[1]
    depth = groups * sum(rows for _, rows in spans)
    args = [packs[j][k] for k in range(groups) for j in range(len(spans))] + list(cots) + list(olds)
    return pl.pallas_call(
        functools.partial(sum_kernel, groups, spans, not olds),
        out_shape=[
            jax.ShapeDtypeStruct((width, rank), jnp.float32),
            jax.ShapeDtypeStruct((rank, width), jnp.float32),
        ],
        in_specs=[VMEM] * len(args),
        out_specs=[VMEM, VMEM],
        scratch_shapes=[
            pltpu.VMEM((depth, width + 2 * rank), jnp.bfloat16),
            pltpu.VMEM((depth, width), jnp.bfloat16),
        ],
        compiler_params=PARAMS,
    )(*args)


def per_device(stash_held, grad_in, w_down, w_up, gain):
    sections = lax.axis_size("pipe")
    groups = lax.axis_size("dp")
    me = lax.axis_index("dp")
    stash, cot, down, upper = stash_held[0], grad_in[0], w_down[0], w_up[0]
    tokens, features = cot.shape
    rank = down.shape[1]
    width = features // groups
    sizes = [tokens * share // sum(SHARES) for share in SHARES]
    spans = [(sum(sizes[:i]), size) for i, size in enumerate(sizes)]
    chunks = len(spans)

    def held(value):
        return exchanged(value, "pipe", sections // 2)

    arrivals = [held(stash[start : start + rows]) for start, rows in spans[:AHEAD]]
    cot_all = []
    for k in range(groups):
        part = lax.dynamic_slice_in_dim(cot, (me ^ k) * width, width, axis=1)
        cot_all.append(exchanged(part, "dp", k) if k else part)
    dact = last_dot(cot, upper)
    index = jnp.reshape(me.astype(jnp.int32), (1,))

    before, packs, partial = [], [], []
    waits = list(cot_all[1:])
    for i, (start, rows) in enumerate(spans):
        following = spans[i + AHEAD] if i + AHEAD < chunks else None
        if i == chunks - 1:
            partial = run_sum(packs, cot_all, spans[:-1], [], rank)
            waits = list(partial) + before[:-1]
        dx, pack, coming = run_chunk(
            index, arrivals[i], cot, dact, down, gain, stash, start, following, waits, groups
        )
        if following:
            arrivals.append(held(coming[0]))
        packs.append([exchanged(pack[k], "dp", k) if k else pack[k] for k in range(groups)])
        before.append(to_previous(dx, "pipe"))
        waits = list(packs[-1][1:]) + before[-1:]
    down_grad, up_grad = run_sum(packs[-1:], cot_all, spans[-1:], partial, rank)
    return (jnp.concatenate(before, axis=0)[None], down_grad[None], up_grad[None])


def solution(mesh):
    in_specs = (
        P("pipe", "dp", None),
        P("pipe", "dp", None),
        P("pipe", None, None),
        P("pipe", None, None),
        P("pipe", None),
    )
    out_specs = (P("pipe", "dp", None), P("pipe", "dp", None), P("pipe", None, "dp"))
    return jax.shard_map(
        per_device, mesh=mesh, in_specs=in_specs, out_specs=out_specs, check_vma=False
    )
```

```python
import functools
import math
import jax
import jax.numpy as jnp
from jax import lax
from jax.experimental import pallas as pl
from jax.experimental.pallas import tpu as pltpu
from jax.sharding import PartitionSpec as P

SHARES = (2, 2, 2, 2)
LANES = 512
VMEM = pl.BlockSpec(memory_space=pltpu.VMEM)
SMEM = pl.BlockSpec(memory_space=pltpu.SMEM)
ANY = pl.BlockSpec(memory_space=pl.ANY)
PARAMS = pltpu.CompilerParams(vmem_limit_bytes=32 * 1024 * 1024)


def exchanged(x, axis, mask):
    return lax.ppermute(x, axis, [(i, i ^ mask) for i in range(lax.axis_size(axis))])


def to_previous(x, axis):
    return lax.ppermute(x, axis, [(i, i - 1) for i in range(1, lax.axis_size(axis))])


def rows_dot(a, b):
    return lax.dot_general(a, b, (((0,), (0,)), ((), ())), preferred_element_type=jnp.float32)


def last_dot(a, b):
    return lax.dot_general(a, b, (((1,), (1,)), ((), ())), preferred_element_type=jnp.float32)


def gelu_and_slope(x):
    c = math.sqrt(2.0 / math.pi)
    th = jnp.tanh(c * (x + 0.044715 * (x * x * x)))
    slope = 0.5 * (1.0 + th) + 0.5 * x * (1.0 - th * th) * (c * (1.0 + 3.0 * 0.044715 * (x * x)))
    return 0.5 * x * (1.0 + th), slope


def copy_kernel(start, stash_ref, *refs):
    out_ref, done = refs[-2:]
    copy = pltpu.make_async_copy(stash_ref.at[pl.ds(start, out_ref.shape[0])], out_ref, done)
    copy.start()
    copy.wait()


def rows_after(stash, start, rows, waits):
    return pl.pallas_call(
        functools.partial(copy_kernel, start),
        out_shape=jax.ShapeDtypeStruct((rows, stash.shape[1]), stash.dtype),
        in_specs=[ANY] * (1 + len(waits)),
        out_specs=ANY,
        scratch_shapes=[pltpu.SemaphoreType.DMA],
    )(stash, *waits)


def pass_kernel(value_ref, wait_ref, out_ref):
    pass


def after(value, wait):
    return pl.pallas_call(
        pass_kernel,
        out_shape=jax.ShapeDtypeStruct(value.shape, value.dtype),
        in_specs=[ANY, ANY],
        out_specs=ANY,
        input_output_aliases={0: 0},
    )(value, wait)


def chunk_kernel(groups, start, waits, me_ref, saved_ref, cot_ref, dact_ref, down_ref, gain_ref, *refs):
    outs = refs[waits:]
    dx_ref, pack_refs, normed_ref = outs[0], outs[1:-1], outs[-1]
    rows, features = saved_ref.shape
    width = features // groups
    rank = down_ref.shape[1]
    lanes = [pl.ds(f, LANES) for f in range(0, features, LANES)]
    total = jnp.zeros((rows, 1), jnp.float32)
    for at in lanes:
        xf = saved_ref[:, at].astype(jnp.float32)
        total += jnp.sum(xf * xf, axis=1, keepdims=True)
    inverse = 1.0 / jnp.sqrt(total / features + 1e-05)
    for at in lanes:
        unit = saved_ref[:, at].astype(jnp.float32) * inverse
        normed_ref[:, at] = (unit * gain_ref[:, at]).astype(jnp.bfloat16)
    pre = jnp.dot(normed_ref[...], down_ref[...], preferred_element_type=jnp.float32)
    act, slope = gelu_and_slope(pre)
    act = act.astype(jnp.bfloat16)
    dpre = (dact_ref[pl.ds(start, rows), :] * slope).astype(jnp.bfloat16)
    inner = jnp.sum(dpre.astype(jnp.float32) * pre, axis=1, keepdims=True) / features
    for k in range(groups):
        at = pl.ds(pl.multiple_of((me_ref[0] ^ k) * width, 128), width)
        pack_refs[k][:, :width] = normed_ref[:, at]
        pack_refs[k][:, width : width + rank] = dpre
        pack_refs[k][:, width + rank :] = act
    pull = inner * inverse
    for at in lanes:
        dnorm = last_dot(dpre, down_ref[at, :]) * gain_ref[:, at]
        xf = saved_ref[:, at].astype(jnp.float32)
        held = cot_ref[pl.ds(start, rows), at].astype(jnp.float32)
        dx_ref[:, at] = (held + (dnorm - xf * pull) * inverse).astype(jnp.bfloat16)


def run_chunk(me, saved, cot, dact, down, gain, start, waits, groups):
    rows, features = saved.shape
    rank = down.shape[1]
    pack = jax.ShapeDtypeStruct((rows, features // groups + 2 * rank), jnp.bfloat16)
    outs = [jax.ShapeDtypeStruct((rows, features), jnp.bfloat16)] + [pack] * groups
    got = pl.pallas_call(
        functools.partial(chunk_kernel, groups, start, len(waits)),
        out_shape=outs,
        in_specs=[SMEM] + [VMEM] * 5 + [ANY] * len(waits),
        out_specs=[VMEM] * len(outs),
        scratch_shapes=[pltpu.VMEM((rows, features), jnp.bfloat16)],
        compiler_params=PARAMS,
    )(me, saved, cot, dact, down, gain, *waits)
    return got[0], got[1:]


def sum_kernel(groups, spans, first, *refs):
    count = groups * len(spans)
    packs, cots = refs[:count], refs[count : count + groups]
    rest = refs[count + groups :]
    if first:
        parts, (down_ref, up_ref, joined, every, held) = rest[: len(spans)], rest[len(spans) :]
        for (start, rows), part in zip(spans, parts):
            joined[pl.ds(start, rows), :] = part[...]
    else:
        olds, (down_ref, up_ref, every, held) = rest[:2], rest[2:]
    width = held.shape[1]
    rank = up_ref.shape[0]
    at = 0
    for k in range(groups):
        for j, (start, rows) in enumerate(spans):
            every[pl.ds(at, rows), :] = packs[k * len(spans) + j][...]
            held[pl.ds(at, rows), :] = cots[k][pl.ds(start, rows), :]
            at += rows
    down = rows_dot(every[:, :width], every[:, width : width + rank])
    up = rows_dot(every[:, width + rank :], held[...])
    down_ref[...] = down if first else down + olds[0][...]
    up_ref[...] = up if first else up + olds[1][...]


def run_sum(packs, cots, spans, others, first, rank):
    groups = len(cots)
    width = cots[0].shape[1]
    depth = groups * sum(rows for _, rows in spans)
    args = [packs[j][k] for k in range(groups) for j in range(len(spans))] + list(cots) + list(others)
    outs = [
        jax.ShapeDtypeStruct((width, rank), jnp.float32),
        jax.ShapeDtypeStruct((rank, width), jnp.float32),
    ]
    if first:
        rows = sum(part.shape[0] for part in others)
        outs.append(jax.ShapeDtypeStruct((rows, others[0].shape[1]), others[0].dtype))
    return pl.pallas_call(
        functools.partial(sum_kernel, groups, spans, first),
        out_shape=outs,
        in_specs=[VMEM] * len(args),
        out_specs=[VMEM] * len(outs),
        scratch_shapes=[
            pltpu.VMEM((depth, width + 2 * rank), jnp.bfloat16),
            pltpu.VMEM((depth, width), jnp.bfloat16),
        ],
        compiler_params=PARAMS,
    )(*args)


def per_device(stash_held, grad_in, w_down, w_up, gain):
    sections = lax.axis_size("pipe")
    groups = lax.axis_size("dp")
    me = lax.axis_index("dp")
    stash, cot, down, upper = stash_held[0], grad_in[0], w_down[0], w_up[0]
    tokens, features = cot.shape
    rank = down.shape[1]
    width = features // groups
    sizes = [tokens * share // sum(SHARES) for share in SHARES]
    spans = [(sum(sizes[:i]), size) for i, size in enumerate(sizes)]
    chunks = len(spans)

    def held(value):
        return exchanged(value, "pipe", sections // 2)

    def coming(i, *waits):
        return held(rows_after(stash, *spans[i], waits))

    arrivals = [held(stash[: sizes[0]])]
    cot_all = []
    for k in range(groups):
        part = lax.dynamic_slice_in_dim(cot, (me ^ k) * width, width, axis=1)
        cot_all.append(exchanged(part, "dp", k) if k else part)
    dact = last_dot(cot, upper)
    arrivals.append(coming(1, cot_all[0]))
    index = jnp.reshape(me.astype(jnp.int32), (1,))

    parts, packs, waits = [], [], cot_all[1:]
    for i, (start, rows) in enumerate(spans):
        if i + 2 < chunks:
            arrivals.append(coming(i + 2, arrivals[i], *parts[-1:]))
        if i == chunks - 1:
            *partial, joined = run_sum(packs, cot_all, spans[:-1], parts, True, rank)
            first = to_previous(after(joined, arrivals[i]), "pipe")
            waits = partial
        dx, pack = run_chunk(index, arrivals[i], cot, dact, down, gain, start, waits, groups)
        packs.append([exchanged(pack[k], "dp", k) if k else pack[k] for k in range(groups)])
        parts.append(dx)
        waits = packs[-1][1:]
    last = to_previous(parts[-1], "pipe")
    down_grad, up_grad = run_sum(packs[-1:], cot_all, spans[-1:], partial, False, rank)
    return (jnp.concatenate([first, last], axis=0)[None], down_grad[None], up_grad[None])


def solution(mesh):
    in_specs = (
        P("pipe", "dp", None),
        P("pipe", "dp", None),
        P("pipe", None, None),
        P("pipe", None, None),
        P("pipe", None),
    )
    out_specs = (P("pipe", "dp", None), P("pipe", "dp", None), P("pipe", None, "dp"))
    return jax.shard_map(
        per_device, mesh=mesh, in_specs=in_specs, out_specs=out_specs, check_vma=False
    )
```

```python
import functools
import math
import jax
import jax.numpy as jnp
from jax import lax
from jax.experimental import pallas as pl
from jax.experimental.pallas import tpu as pltpu
from jax.sharding import PartitionSpec as P

SHARES = (2, 2, 2, 2)
LANES = 512
VMEM = pl.BlockSpec(memory_space=pltpu.VMEM)
SMEM = pl.BlockSpec(memory_space=pltpu.SMEM)
ANY = pl.BlockSpec(memory_space=pl.ANY)
PARAMS = pltpu.CompilerParams(vmem_limit_bytes=16 * 1024 * 1024)
SMALL = pltpu.CompilerParams(vmem_limit_bytes=4 * 1024 * 1024)


def exchanged(x, axis, mask):
    return lax.ppermute(x, axis, [(i, i ^ mask) for i in range(lax.axis_size(axis))])


def to_previous(x, axis):
    return lax.ppermute(x, axis, [(i, i - 1) for i in range(1, lax.axis_size(axis))])


def rows_dot(a, b):
    return lax.dot_general(a, b, (((0,), (0,)), ((), ())), preferred_element_type=jnp.float32)


def last_dot(a, b):
    return lax.dot_general(a, b, (((1,), (1,)), ((), ())), preferred_element_type=jnp.float32)


def gelu_and_slope(x):
    c = math.sqrt(2.0 / math.pi)
    th = jnp.tanh(c * (x + 0.044715 * (x * x * x)))
    slope = 0.5 * (1.0 + th) + 0.5 * x * (1.0 - th * th) * (c * (1.0 + 3.0 * 0.044715 * (x * x)))
    return 0.5 * x * (1.0 + th), slope


def copy_kernel(start, stash_ref, *refs):
    out_ref, done = refs[-2:]
    copy = pltpu.make_async_copy(stash_ref.at[pl.ds(start, out_ref.shape[0])], out_ref, done)
    copy.start()
    copy.wait()


def rows_after(stash, start, rows, waits):
    return pl.pallas_call(
        functools.partial(copy_kernel, start),
        out_shape=jax.ShapeDtypeStruct((rows, stash.shape[1]), stash.dtype),
        in_specs=[ANY] * (1 + len(waits)),
        out_specs=VMEM,
        scratch_shapes=[pltpu.SemaphoreType.DMA],
        compiler_params=SMALL,
    )(stash, *waits)


def pass_kernel(value_ref, wait_ref, out_ref):
    pass


def after(value, wait):
    return pl.pallas_call(
        pass_kernel,
        out_shape=jax.ShapeDtypeStruct(value.shape, value.dtype),
        in_specs=[ANY, ANY],
        out_specs=ANY,
        input_output_aliases={0: 0},
        compiler_params=SMALL,
    )(value, wait)


def chunk_kernel(groups, start, waits, me_ref, saved_ref, cot_ref, dact_ref, down_ref, gain_ref, *refs):
    outs = refs[waits:]
    dx_ref, pack_refs, normed_ref = outs[0], outs[1:-1], outs[-1]
    rows, features = saved_ref.shape
    width = features // groups
    rank = down_ref.shape[1]
    lanes = [pl.ds(f, LANES) for f in range(0, features, LANES)]
    total = jnp.zeros((rows, 1), jnp.float32)
    for at in lanes:
        xf = saved_ref[:, at].astype(jnp.float32)
        total += jnp.sum(xf * xf, axis=1, keepdims=True)
    inverse = 1.0 / jnp.sqrt(total / features + 1e-05)
    for at in lanes:
        unit = saved_ref[:, at].astype(jnp.float32) * inverse
        normed_ref[:, at] = (unit * gain_ref[:, at]).astype(jnp.bfloat16)
    pre = jnp.dot(normed_ref[...], down_ref[...], preferred_element_type=jnp.float32)
    act, slope = gelu_and_slope(pre)
    act = act.astype(jnp.bfloat16)
    dpre = (dact_ref[pl.ds(start, rows), :] * slope).astype(jnp.bfloat16)
    inner = jnp.sum(dpre.astype(jnp.float32) * pre, axis=1, keepdims=True) / features
    for k in range(groups):
        at = pl.ds(pl.multiple_of((me_ref[0] ^ k) * width, 128), width)
        pack_refs[k][:, :width] = normed_ref[:, at]
        pack_refs[k][:, width : width + rank] = dpre
        pack_refs[k][:, width + rank :] = act
    pull = inner * inverse
    for at in lanes:
        dnorm = last_dot(dpre, down_ref[at, :]) * gain_ref[:, at]
        xf = saved_ref[:, at].astype(jnp.float32)
        held = cot_ref[pl.ds(start, rows), at].astype(jnp.float32)
        dx_ref[:, at] = (held + (dnorm - xf * pull) * inverse).astype(jnp.bfloat16)


def run_chunk(me, saved, cot, dact, down, gain, start, waits, groups):
    rows, features = saved.shape
    rank = down.shape[1]
    pack = jax.ShapeDtypeStruct((rows, features // groups + 2 * rank), jnp.bfloat16)
    outs = [jax.ShapeDtypeStruct((rows, features), jnp.bfloat16)] + [pack] * groups
    got = pl.pallas_call(
        functools.partial(chunk_kernel, groups, start, len(waits)),
        out_shape=outs,
        in_specs=[SMEM] + [VMEM] * 5 + [ANY] * len(waits),
        out_specs=[VMEM] * len(outs),
        scratch_shapes=[pltpu.VMEM((rows, features), jnp.bfloat16)],
        compiler_params=PARAMS,
    )(me, saved, cot, dact, down, gain, *waits)
    return got[0], got[1:]


def sum_kernel(groups, spans, first, *refs):
    count = groups * len(spans)
    packs, cots = refs[:count], refs[count : count + groups]
    rest = refs[count + groups :]
    if first:
        parts, (down_ref, up_ref, joined, every, held) = rest[: len(spans)], rest[len(spans) :]
        for (start, rows), part in zip(spans, parts):
            joined[pl.ds(start, rows), :] = part[...]
    else:
        olds, (down_ref, up_ref, every, held) = rest[:2], rest[2:]
    width = held.shape[1]
    rank = up_ref.shape[0]
    at = 0
    for k in range(groups):
        for j, (start, rows) in enumerate(spans):
            every[pl.ds(at, rows), :] = packs[k * len(spans) + j][...]
            held[pl.ds(at, rows), :] = cots[k][pl.ds(start, rows), :]
            at += rows
    down = rows_dot(every[:, :width], every[:, width : width + rank])
    up = rows_dot(every[:, width + rank :], held[...])
    down_ref[...] = down if first else down + olds[0][...]
    up_ref[...] = up if first else up + olds[1][...]


def run_sum(packs, cots, spans, others, first, rank):
    groups = len(cots)
    width = cots[0].shape[1]
    depth = groups * sum(rows for _, rows in spans)
    args = [packs[j][k] for k in range(groups) for j in range(len(spans))] + list(cots) + list(others)
    outs = [
        jax.ShapeDtypeStruct((width, rank), jnp.float32),
        jax.ShapeDtypeStruct((rank, width), jnp.float32),
    ]
    if first:
        rows = sum(part.shape[0] for part in others)
        outs.append(jax.ShapeDtypeStruct((rows, others[0].shape[1]), others[0].dtype))
    return pl.pallas_call(
        functools.partial(sum_kernel, groups, spans, first),
        out_shape=outs,
        in_specs=[VMEM] * len(args),
        out_specs=[VMEM] * len(outs),
        scratch_shapes=[
            pltpu.VMEM((depth, width + 2 * rank), jnp.bfloat16),
            pltpu.VMEM((depth, width), jnp.bfloat16),
        ],
        compiler_params=PARAMS,
    )(*args)


def per_device(stash_held, grad_in, w_down, w_up, gain):
    sections = lax.axis_size("pipe")
    groups = lax.axis_size("dp")
    me = lax.axis_index("dp")
    stash, cot, down, upper = stash_held[0], grad_in[0], w_down[0], w_up[0]
    tokens, features = cot.shape
    rank = down.shape[1]
    width = features // groups
    sizes = [tokens * share // sum(SHARES) for share in SHARES]
    spans = [(sum(sizes[:i]), size) for i, size in enumerate(sizes)]
    chunks = len(spans)

    def held(value):
        return exchanged(value, "pipe", sections // 2)

    def coming(i, *waits):
        return held(rows_after(stash, *spans[i], waits))

    arrivals = [held(stash[: sizes[0]])]
    cot_all = []
    for k in range(groups):
        part = lax.dynamic_slice_in_dim(cot, (me ^ k) * width, width, axis=1)
        cot_all.append(exchanged(part, "dp", k) if k else part)
    dact = last_dot(cot, upper)
    arrivals.append(coming(1, cot_all[0]))
    index = jnp.reshape(me.astype(jnp.int32), (1,))

    parts, packs, waits = [], [], cot_all[1:]
    for i, (start, rows) in enumerate(spans):
        if i + 2 < chunks:
            arrivals.append(coming(i + 2, arrivals[i], *parts[-1:]))
        if i == chunks - 1:
            *partial, joined = run_sum(packs, cot_all, spans[:-1], parts, True, rank)
            first = to_previous(after(joined, arrivals[i]), "pipe")
            waits = partial
        dx, pack = run_chunk(index, arrivals[i], cot, dact, down, gain, start, waits, groups)
        packs.append([exchanged(pack[k], "dp", k) if k else pack[k] for k in range(groups)])
        parts.append(dx)
        waits = packs[-1][1:]
    last = to_previous(parts[-1], "pipe")
    down_grad, up_grad = run_sum(packs[-1:], cot_all, spans[-1:], partial, False, rank)
    return (jnp.concatenate([first, last], axis=0)[None], down_grad[None], up_grad[None])


def solution(mesh):
    in_specs = (
        P("pipe", "dp", None),
        P("pipe", "dp", None),
        P("pipe", None, None),
        P("pipe", None, None),
        P("pipe", None),
    )
    out_specs = (P("pipe", "dp", None), P("pipe", "dp", None), P("pipe", None, "dp"))
    return jax.shard_map(
        per_device, mesh=mesh, in_specs=in_specs, out_specs=out_specs, check_vma=False
    )
```

```python
import functools
import math
import jax
import jax.numpy as jnp
from jax import lax
from jax.experimental import pallas as pl
from jax.experimental.pallas import tpu as pltpu
from jax.sharding import PartitionSpec as P

SHARES = (1, 2, 2, 3)
LANES = 512
VMEM = pl.BlockSpec(memory_space=pltpu.VMEM)
SMEM = pl.BlockSpec(memory_space=pltpu.SMEM)
ANY = pl.BlockSpec(memory_space=pl.ANY)
PARAMS = pltpu.CompilerParams(vmem_limit_bytes=16 * 1024 * 1024)
SMALL = pltpu.CompilerParams(vmem_limit_bytes=4 * 1024 * 1024)


def exchanged(x, axis, mask):
    return lax.ppermute(x, axis, [(i, i ^ mask) for i in range(lax.axis_size(axis))])


def to_previous(x, axis):
    return lax.ppermute(x, axis, [(i, i - 1) for i in range(1, lax.axis_size(axis))])


def rows_dot(a, b):
    return lax.dot_general(a, b, (((0,), (0,)), ((), ())), preferred_element_type=jnp.float32)


def last_dot(a, b):
    return lax.dot_general(a, b, (((1,), (1,)), ((), ())), preferred_element_type=jnp.float32)


def gelu_and_slope(x):
    c = math.sqrt(2.0 / math.pi)
    th = jnp.tanh(c * (x + 0.044715 * (x * x * x)))
    slope = 0.5 * (1.0 + th) + 0.5 * x * (1.0 - th * th) * (c * (1.0 + 3.0 * 0.044715 * (x * x)))
    return 0.5 * x * (1.0 + th), slope


def copy_kernel(start, stash_ref, *refs):
    out_ref, done = refs[-2:]
    copy = pltpu.make_async_copy(stash_ref.at[pl.ds(start, out_ref.shape[0])], out_ref, done)
    copy.start()
    copy.wait()


def rows_after(stash, start, rows, waits):
    return pl.pallas_call(
        functools.partial(copy_kernel, start),
        out_shape=jax.ShapeDtypeStruct((rows, stash.shape[1]), stash.dtype),
        in_specs=[ANY] * (1 + len(waits)),
        out_specs=VMEM,
        scratch_shapes=[pltpu.SemaphoreType.DMA],
        compiler_params=SMALL,
    )(stash, *waits)


def chunk_kernel(groups, start, waits, me_ref, saved_ref, cot_ref, dact_ref, down_ref, gain_ref, *refs):
    outs = refs[waits:]
    dx_ref, pack_refs, normed_ref = outs[0], outs[1:-1], outs[-1]
    rows, features = saved_ref.shape
    width = features // groups
    rank = down_ref.shape[1]
    lanes = [pl.ds(f, LANES) for f in range(0, features, LANES)]
    total = jnp.zeros((rows, 1), jnp.float32)
    for at in lanes:
        xf = saved_ref[:, at].astype(jnp.float32)
        total += jnp.sum(xf * xf, axis=1, keepdims=True)
    inverse = 1.0 / jnp.sqrt(total / features + 1e-05)
    for at in lanes:
        unit = saved_ref[:, at].astype(jnp.float32) * inverse
        normed_ref[:, at] = (unit * gain_ref[:, at]).astype(jnp.bfloat16)
    pre = jnp.dot(normed_ref[...], down_ref[...], preferred_element_type=jnp.float32)
    act, slope = gelu_and_slope(pre)
    act = act.astype(jnp.bfloat16)
    dpre = (dact_ref[pl.ds(start, rows), :] * slope).astype(jnp.bfloat16)
    inner = jnp.sum(dpre.astype(jnp.float32) * pre, axis=1, keepdims=True) / features
    for k in range(groups):
        at = pl.ds(pl.multiple_of((me_ref[0] ^ k) * width, 128), width)
        pack_refs[k][:, :width] = normed_ref[:, at]
        pack_refs[k][:, width : width + rank] = dpre
        pack_refs[k][:, width + rank :] = act
    pull = inner * inverse
    for at in lanes:
        dnorm = last_dot(dpre, down_ref[at, :]) * gain_ref[:, at]
        xf = saved_ref[:, at].astype(jnp.float32)
        held = cot_ref[pl.ds(start, rows), at].astype(jnp.float32)
        dx_ref[:, at] = (held + (dnorm - xf * pull) * inverse).astype(jnp.bfloat16)


def run_chunk(me, saved, cot, dact, down, gain, start, waits, groups):
    rows, features = saved.shape
    rank = down.shape[1]
    pack = jax.ShapeDtypeStruct((rows, features // groups + 2 * rank), jnp.bfloat16)
    outs = [jax.ShapeDtypeStruct((rows, features), jnp.bfloat16)] + [pack] * groups
    got = pl.pallas_call(
        functools.partial(chunk_kernel, groups, start, len(waits)),
        out_shape=outs,
        in_specs=[SMEM] + [VMEM] * 5 + [ANY] * len(waits),
        out_specs=[VMEM] * len(outs),
        scratch_shapes=[pltpu.VMEM((rows, features), jnp.bfloat16)],
        compiler_params=PARAMS,
    )(me, saved, cot, dact, down, gain, *waits)
    return got[0], got[1:]


def gather_rows(groups, spans, packs, cots, every, held):
    at = 0
    for k in range(groups):
        for j, (start, rows) in enumerate(spans):
            every[pl.ds(at, rows), :] = packs[k * len(spans) + j][...]
            held[pl.ds(at, rows), :] = cots[k][pl.ds(start, rows), :]
            at += rows


def sum_kernel(groups, spans, *refs):
    count = groups * len(spans)
    packs, cots, parts = refs[:count], refs[count : count + groups], refs[count + groups : -5]
    down_ref, up_ref, joined, every, held = refs[-5:]
    width, rank = down_ref.shape
    gather_rows(groups, spans, packs, cots, every, held)
    down_ref[...] = rows_dot(every[:, :width], every[:, width : width + rank])
    up_ref[...] = rows_dot(every[:, width + rank :], held[...])
    for (start, rows), part in zip(spans, parts):
        joined[pl.ds(start, rows), :] = part[...]


def final_kernel(groups, spans, *refs):
    packs, cots = refs[:groups], refs[groups : 2 * groups]
    old_down, old_up, first, last = refs[2 * groups : 2 * groups + 4]
    before_ref, down_ref, up_ref, every, held, down, up, done = refs[2 * groups + 4 :]
    width, rank = down.shape
    rows = first.shape[0]
    copies = [
        pltpu.make_async_copy(first, before_ref.at[pl.ds(0, rows)], done.at[0]),
        pltpu.make_async_copy(last, before_ref.at[pl.ds(rows, last.shape[0])], done.at[1]),
        pltpu.make_async_copy(down, down_ref, done.at[2]),
        pltpu.make_async_copy(up, up_ref, done.at[3]),
    ]
    copies[0].start()
    copies[1].start()
    gather_rows(groups, spans, packs, cots, every, held)
    down[...] = old_down[...] + rows_dot(every[:, :width], every[:, width : width + rank])
    copies[2].start()
    up[...] = old_up[...] + rows_dot(every[:, width + rank :], held[...])
    copies[3].start()
    for copy in copies:
        copy.wait()


def operands(packs, cots, spans):
    groups = len(cots)
    width = cots[0].shape[1]
    depth = groups * sum(rows for _, rows in spans)
    args = [packs[j][k] for k in range(groups) for j in range(len(spans))] + list(cots)
    scratch = [
        pltpu.VMEM((depth, packs[0][0].shape[1]), jnp.bfloat16),
        pltpu.VMEM((depth, width), jnp.bfloat16),
    ]
    return groups, width, args, scratch


def run_sum(packs, cots, spans, parts, rank):
    groups, width, args, scratch = operands(packs, cots, spans)
    args += parts
    rows = sum(part.shape[0] for part in parts)
    return pl.pallas_call(
        functools.partial(sum_kernel, groups, spans),
        out_shape=[
            jax.ShapeDtypeStruct((width, rank), jnp.float32),
            jax.ShapeDtypeStruct((rank, width), jnp.float32),
            jax.ShapeDtypeStruct((rows, parts[0].shape[1]), jnp.bfloat16),
        ],
        in_specs=[VMEM] * len(args),
        out_specs=[VMEM] * 3,
        scratch_shapes=scratch,
        compiler_params=PARAMS,
    )(*args)


def run_final(packs, cots, spans, partial, first, last):
    groups, width, args, scratch = operands(packs, cots, spans)
    down, up = partial
    args += [down, up, first, last]
    before = jax.ShapeDtypeStruct((first.shape[0] + last.shape[0], first.shape[1]), jnp.bfloat16)
    scratch += [
        pltpu.VMEM(down.shape, jnp.float32),
        pltpu.VMEM(up.shape, jnp.float32),
        pltpu.SemaphoreType.DMA((4,)),
    ]
    return pl.pallas_call(
        functools.partial(final_kernel, groups, spans),
        out_shape=[
            before,
            jax.ShapeDtypeStruct(down.shape, jnp.float32),
            jax.ShapeDtypeStruct(up.shape, jnp.float32),
        ],
        in_specs=[VMEM] * len(args),
        out_specs=[ANY] * 3,
        scratch_shapes=scratch,
        compiler_params=PARAMS,
    )(*args)


def per_device(stash_held, grad_in, w_down, w_up, gain):
    sections = lax.axis_size("pipe")
    groups = lax.axis_size("dp")
    me = lax.axis_index("dp")
    stash, cot, down, upper = stash_held[0], grad_in[0], w_down[0], w_up[0]
    tokens, features = cot.shape
    rank = down.shape[1]
    width = features // groups
    sizes = [tokens * share // sum(SHARES) for share in SHARES]
    spans = [(sum(sizes[:i]), size) for i, size in enumerate(sizes)]
    chunks = len(spans)

    def held(value):
        return exchanged(value, "pipe", sections // 2)

    arrivals = [held(stash[start : start + rows]) for start, rows in spans[:2]]
    cot_all = []
    for k in range(groups):
        part = lax.dynamic_slice_in_dim(cot, (me ^ k) * width, width, axis=1)
        cot_all.append(exchanged(part, "dp", k) if k else part)
    dact = last_dot(cot, upper)
    index = jnp.reshape(me.astype(jnp.int32), (1,))

    parts, packs, waits = [], [], cot_all[1:]
    for i, (start, rows) in enumerate(spans):
        if i + 2 < chunks:
            coming = rows_after(stash, *spans[i + 2], [arrivals[i]] + waits * (i > 0))
            arrivals.append(held(coming))
            waits = waits + [coming]
        if i == chunks - 1:
            *partial, joined = run_sum(packs, cot_all, spans[:-1], parts, rank)
            first = to_previous(joined, "pipe")
            waits = partial
        dx, pack = run_chunk(index, arrivals[i], cot, dact, down, gain, start, waits, groups)
        packs.append([exchanged(pack[k], "dp", k) if k else pack[k] for k in range(groups)])
        parts.append(dx)
        waits = packs[-1][1:]
    last = to_previous(parts[-1], "pipe")
    before, down_grad, up_grad = run_final(packs[-1:], cot_all, spans[-1:], partial, first, last)
    return (before[None], down_grad[None], up_grad[None])


def solution(mesh):
    in_specs = (
        P("pipe", "dp", None),
        P("pipe", "dp", None),
        P("pipe", None, None),
        P("pipe", None, None),
        P("pipe", None),
    )
    out_specs = (P("pipe", "dp", None), P("pipe", "dp", None), P("pipe", None, "dp"))
    return jax.shard_map(
        per_device, mesh=mesh, in_specs=in_specs, out_specs=out_specs, check_vma=False
    )
```

```python
import functools
import math
import jax
import jax.numpy as jnp
from jax import lax
from jax.experimental import pallas as pl
from jax.experimental.pallas import tpu as pltpu
from jax.sharding import PartitionSpec as P

SHARES = (1, 2, 2, 3)
LANES = 512
VMEM = pl.BlockSpec(memory_space=pltpu.VMEM)
SMEM = pl.BlockSpec(memory_space=pltpu.SMEM)
ANY = pl.BlockSpec(memory_space=pl.ANY)
PARAMS = pltpu.CompilerParams(vmem_limit_bytes=16 * 1024 * 1024)
SMALL = pltpu.CompilerParams(vmem_limit_bytes=4 * 1024 * 1024)


def exchanged(x, axis, mask):
    return lax.ppermute(x, axis, [(i, i ^ mask) for i in range(lax.axis_size(axis))])


def to_previous(x, axis):
    return lax.ppermute(x, axis, [(i, i - 1) for i in range(1, lax.axis_size(axis))])


def rows_dot(a, b):
    return lax.dot_general(a, b, (((0,), (0,)), ((), ())), preferred_element_type=jnp.float32)


def last_dot(a, b):
    return lax.dot_general(a, b, (((1,), (1,)), ((), ())), preferred_element_type=jnp.float32)


def gelu_and_slope(x):
    c = math.sqrt(2.0 / math.pi)
    th = jnp.tanh(c * (x + 0.044715 * (x * x * x)))
    slope = 0.5 * (1.0 + th) + 0.5 * x * (1.0 - th * th) * (c * (1.0 + 3.0 * 0.044715 * (x * x)))
    return 0.5 * x * (1.0 + th), slope


def copy_kernel(start, stash_ref, *refs):
    out_ref, done = refs[-2:]
    copy = pltpu.make_async_copy(stash_ref.at[pl.ds(start, out_ref.shape[0])], out_ref, done)
    copy.start()
    copy.wait()


def rows_after(stash, start, rows, waits):
    return pl.pallas_call(
        functools.partial(copy_kernel, start),
        out_shape=jax.ShapeDtypeStruct((rows, stash.shape[1]), stash.dtype),
        in_specs=[ANY] * (1 + len(waits)),
        out_specs=VMEM,
        scratch_shapes=[pltpu.SemaphoreType.DMA],
        compiler_params=SMALL,
    )(stash, *waits)


def chunk_kernel(start, joins, waits, me_ref, saved_ref, cot_ref, dact_ref, down_ref, gain_ref, *refs):
    outs = refs[joins + waits :]
    dx_ref, pack_refs, normed_ref = outs[0], outs[1:-1], outs[-1]
    groups = len(pack_refs)
    rows, features = saved_ref.shape
    ahead = dx_ref.shape[0] - rows
    at = 0
    for part in refs[:joins]:
        dx_ref[pl.ds(at, part.shape[0]), :] = part[...]
        at += part.shape[0]
    width = features // groups
    rank = down_ref.shape[1]
    lanes = [pl.ds(f, LANES) for f in range(0, features, LANES)]
    total = jnp.zeros((rows, 1), jnp.float32)
    for at in lanes:
        xf = saved_ref[:, at].astype(jnp.float32)
        total += jnp.sum(xf * xf, axis=1, keepdims=True)
    inverse = 1.0 / jnp.sqrt(total / features + 1e-05)
    for at in lanes:
        unit = saved_ref[:, at].astype(jnp.float32) * inverse
        normed_ref[:, at] = (unit * gain_ref[:, at]).astype(jnp.bfloat16)
    pre = jnp.dot(normed_ref[...], down_ref[...], preferred_element_type=jnp.float32)
    act, slope = gelu_and_slope(pre)
    act = act.astype(jnp.bfloat16)
    dpre = (dact_ref[pl.ds(start, rows), :] * slope).astype(jnp.bfloat16)
    inner = jnp.sum(dpre.astype(jnp.float32) * pre, axis=1, keepdims=True) / features
    for k in range(groups):
        at = pl.ds(pl.multiple_of((me_ref[0] ^ k) * width, 128), width)
        pack_refs[k][:, :width] = normed_ref[:, at]
        pack_refs[k][:, width : width + rank] = dpre
        pack_refs[k][:, width + rank :] = act
    pull = inner * inverse
    for at in lanes:
        dnorm = last_dot(dpre, down_ref[at, :]) * gain_ref[:, at]
        xf = saved_ref[:, at].astype(jnp.float32)
        held = cot_ref[pl.ds(start, rows), at].astype(jnp.float32)
        dx_ref[pl.ds(ahead, rows), at] = (held + (dnorm - xf * pull) * inverse).astype(jnp.bfloat16)


def run_chunk(me, saved, cot, dact, down, gain, start, joins, waits, groups):
    rows, features = saved.shape
    rank = down.shape[1]
    pack = jax.ShapeDtypeStruct((rows, features // groups + 2 * rank), jnp.bfloat16)
    ahead = sum(part.shape[0] for part in joins)
    outs = [jax.ShapeDtypeStruct((ahead + rows, features), jnp.bfloat16)] + [pack] * groups
    got = pl.pallas_call(
        functools.partial(chunk_kernel, start, len(joins), len(waits)),
        out_shape=outs,
        in_specs=[SMEM] + [VMEM] * (5 + len(joins)) + [ANY] * len(waits),
        out_specs=[VMEM] * len(outs),
        scratch_shapes=[pltpu.VMEM((rows, features), jnp.bfloat16)],
        compiler_params=PARAMS,
    )(me, saved, cot, dact, down, gain, *joins, *waits)
    return got[0], got[1:]


def gather_rows(groups, spans, packs, cots, every, held):
    at = 0
    for k in range(groups):
        for j, (start, rows) in enumerate(spans):
            every[pl.ds(at, rows), :] = packs[k * len(spans) + j][...]
            held[pl.ds(at, rows), :] = cots[k][pl.ds(start, rows), :]
            at += rows


def sum_kernel(groups, spans, *refs):
    count = groups * len(spans)
    packs, cots = refs[:count], refs[count : count + groups]
    down_ref, up_ref, every, held = refs[-4:]
    width, rank = down_ref.shape
    gather_rows(groups, spans, packs, cots, every, held)
    down_ref[...] = rows_dot(every[:, :width], every[:, width : width + rank])
    up_ref[...] = rows_dot(every[:, width + rank :], held[...])


def final_kernel(groups, spans, *refs):
    packs, cots = refs[:groups], refs[groups : 2 * groups]
    old_down, old_up, first, last = refs[2 * groups : 2 * groups + 4]
    before_ref, down_ref, up_ref, every, held, down, up, done = refs[2 * groups + 4 :]
    width, rank = down.shape
    rows = first.shape[0]
    copies = [
        pltpu.make_async_copy(first, before_ref.at[pl.ds(0, rows)], done.at[0]),
        pltpu.make_async_copy(last, before_ref.at[pl.ds(rows, last.shape[0])], done.at[1]),
        pltpu.make_async_copy(down, down_ref, done.at[2]),
        pltpu.make_async_copy(up, up_ref, done.at[3]),
    ]
    copies[0].start()
    copies[1].start()
    gather_rows(groups, spans, packs, cots, every, held)
    down[...] = old_down[...] + rows_dot(every[:, :width], every[:, width : width + rank])
    copies[2].start()
    up[...] = old_up[...] + rows_dot(every[:, width + rank :], held[...])
    copies[3].start()
    for copy in copies:
        copy.wait()


def operands(packs, cots, spans):
    groups = len(cots)
    width = cots[0].shape[1]
    depth = groups * sum(rows for _, rows in spans)
    args = [packs[j][k] for k in range(groups) for j in range(len(spans))] + list(cots)
    scratch = [
        pltpu.VMEM((depth, packs[0][0].shape[1]), jnp.bfloat16),
        pltpu.VMEM((depth, width), jnp.bfloat16),
    ]
    return groups, width, args, scratch


def run_sum(packs, cots, spans, waits, rank):
    groups, width, args, scratch = operands(packs, cots, spans)
    return pl.pallas_call(
        functools.partial(sum_kernel, groups, spans),
        out_shape=[
            jax.ShapeDtypeStruct((width, rank), jnp.float32),
            jax.ShapeDtypeStruct((rank, width), jnp.float32),
        ],
        in_specs=[VMEM] * len(args) + [ANY] * len(waits),
        out_specs=[VMEM] * 2,
        scratch_shapes=scratch,
        compiler_params=PARAMS,
    )(*args, *waits)


def run_final(packs, cots, spans, partial, first, last):
    groups, width, args, scratch = operands(packs, cots, spans)
    down, up = partial
    args += [down, up, first, last]
    before = jax.ShapeDtypeStruct((first.shape[0] + last.shape[0], first.shape[1]), jnp.bfloat16)
    scratch += [
        pltpu.VMEM(down.shape, jnp.float32),
        pltpu.VMEM(up.shape, jnp.float32),
        pltpu.SemaphoreType.DMA((4,)),
    ]
    return pl.pallas_call(
        functools.partial(final_kernel, groups, spans),
        out_shape=[
            before,
            jax.ShapeDtypeStruct(down.shape, jnp.float32),
            jax.ShapeDtypeStruct(up.shape, jnp.float32),
        ],
        in_specs=[VMEM] * len(args),
        out_specs=[ANY] * 3,
        scratch_shapes=scratch,
        compiler_params=PARAMS,
    )(*args)


def per_device(stash_held, grad_in, w_down, w_up, gain):
    sections = lax.axis_size("pipe")
    groups = lax.axis_size("dp")
    me = lax.axis_index("dp")
    stash, cot, down, upper = stash_held[0], grad_in[0], w_down[0], w_up[0]
    tokens, features = cot.shape
    rank = down.shape[1]
    width = features // groups
    sizes = [tokens * share // sum(SHARES) for share in SHARES]
    spans = [(sum(sizes[:i]), size) for i, size in enumerate(sizes)]
    chunks = len(spans)

    def held(value):
        return exchanged(value, "pipe", sections // 2)

    arrivals = [held(stash[start : start + rows]) for start, rows in spans[:2]]
    cot_all = []
    for k in range(groups):
        part = lax.dynamic_slice_in_dim(cot, (me ^ k) * width, width, axis=1)
        cot_all.append(exchanged(part, "dp", k) if k else part)
    dact = last_dot(cot, upper)
    index = jnp.reshape(me.astype(jnp.int32), (1,))

    parts, packs, waits = [], [], cot_all[1:]
    for i, (start, rows) in enumerate(spans):
        if i + 2 < chunks:
            coming = rows_after(stash, *spans[i + 2], [arrivals[i]] + waits * (i > 0))
            arrivals.append(held(coming))
            waits = waits + [coming]
        joins = parts if i == chunks - 2 else []
        dx, pack = run_chunk(index, arrivals[i], cot, dact, down, gain, start, joins, waits, groups)
        packs.append([exchanged(pack[k], "dp", k) if k else pack[k] for k in range(groups)])
        parts.append(dx)
        waits = packs[-1][1:]
    partial = run_sum(packs[:-1], cot_all, spans[:-1], [pack[0]], rank)
    first, last = [to_previous(dx, "pipe") for dx in parts[-2:]]
    before, down_grad, up_grad = run_final(packs[-1:], cot_all, spans[-1:], partial, first, last)
    return (before[None], down_grad[None], up_grad[None])


def solution(mesh):
    in_specs = (
        P("pipe", "dp", None),
        P("pipe", "dp", None),
        P("pipe", None, None),
        P("pipe", None, None),
        P("pipe", None),
    )
    out_specs = (P("pipe", "dp", None), P("pipe", "dp", None), P("pipe", None, "dp"))
    return jax.shard_map(
        per_device, mesh=mesh, in_specs=in_specs, out_specs=out_specs, check_vma=False
    )
```

```python
import functools
import math
import jax
import jax.numpy as jnp
from jax import lax
from jax.experimental import pallas as pl
from jax.experimental.pallas import tpu as pltpu
from jax.sharding import PartitionSpec as P

SHARES = (3, 2, 3)
LANES = 512
VMEM = pl.BlockSpec(memory_space=pltpu.VMEM)
SMEM = pl.BlockSpec(memory_space=pltpu.SMEM)
ANY = pl.BlockSpec(memory_space=pl.ANY)
PARAMS = pltpu.CompilerParams(vmem_limit_bytes=16 * 1024 * 1024)
SMALL = pltpu.CompilerParams(vmem_limit_bytes=4 * 1024 * 1024)


def exchanged(x, axis, mask):
    return lax.ppermute(x, axis, [(i, i ^ mask) for i in range(lax.axis_size(axis))])


def to_previous(x, axis):
    return lax.ppermute(x, axis, [(i, i - 1) for i in range(1, lax.axis_size(axis))])


def rows_dot(a, b):
    return lax.dot_general(a, b, (((0,), (0,)), ((), ())), preferred_element_type=jnp.float32)


def last_dot(a, b):
    return lax.dot_general(a, b, (((1,), (1,)), ((), ())), preferred_element_type=jnp.float32)


def gelu_and_slope(x):
    c = math.sqrt(2.0 / math.pi)
    th = jnp.tanh(c * (x + 0.044715 * (x * x * x)))
    slope = 0.5 * (1.0 + th) + 0.5 * x * (1.0 - th * th) * (c * (1.0 + 3.0 * 0.044715 * (x * x)))
    return 0.5 * x * (1.0 + th), slope


def copy_kernel(start, stash_ref, *refs):
    out_ref, done = refs[-2:]
    copy = pltpu.make_async_copy(stash_ref.at[pl.ds(start, out_ref.shape[0])], out_ref, done)
    copy.start()
    copy.wait()


def rows_after(stash, start, rows, waits):
    return pl.pallas_call(
        functools.partial(copy_kernel, start),
        out_shape=jax.ShapeDtypeStruct((rows, stash.shape[1]), stash.dtype),
        in_specs=[ANY] * (1 + len(waits)),
        out_specs=VMEM,
        scratch_shapes=[pltpu.SemaphoreType.DMA],
        compiler_params=SMALL,
    )(stash, *waits)


def chunk_kernel(start, pieces, groups, me_ref, cot_ref, dact_ref, down_ref, gain_ref, *refs):
    saved_ref, normed_ref = refs[-2:]
    dx_ref, pack_refs = refs[-3 - groups], refs[-2 - groups : -2]
    at = 0
    for piece in refs[:pieces]:
        saved_ref[pl.ds(at, piece.shape[0]), :] = piece[...]
        at += piece.shape[0]
    rows, features = saved_ref.shape
    width = features // groups
    rank = down_ref.shape[1]
    lanes = [pl.ds(f, LANES) for f in range(0, features, LANES)]
    total = jnp.zeros((rows, 1), jnp.float32)
    for at in lanes:
        xf = saved_ref[:, at].astype(jnp.float32)
        total += jnp.sum(xf * xf, axis=1, keepdims=True)
    inverse = 1.0 / jnp.sqrt(total / features + 1e-05)
    for at in lanes:
        unit = saved_ref[:, at].astype(jnp.float32) * inverse
        normed_ref[:, at] = (unit * gain_ref[:, at]).astype(jnp.bfloat16)
    pre = jnp.dot(normed_ref[...], down_ref[...], preferred_element_type=jnp.float32)
    act, slope = gelu_and_slope(pre)
    act = act.astype(jnp.bfloat16)
    dpre = (dact_ref[pl.ds(start, rows), :] * slope).astype(jnp.bfloat16)
    inner = jnp.sum(dpre.astype(jnp.float32) * pre, axis=1, keepdims=True) / features
    for k in range(groups):
        at = pl.ds(pl.multiple_of((me_ref[0] ^ k) * width, 128), width)
        pack_refs[k][:, :width] = normed_ref[:, at]
        pack_refs[k][:, width : width + rank] = dpre
        pack_refs[k][:, width + rank :] = act
    pull = inner * inverse
    for at in lanes:
        dnorm = last_dot(dpre, down_ref[at, :]) * gain_ref[:, at]
        xf = saved_ref[:, at].astype(jnp.float32)
        held = cot_ref[pl.ds(start, rows), at].astype(jnp.float32)
        dx_ref[:, at] = (held + (dnorm - xf * pull) * inverse).astype(jnp.bfloat16)


def run_chunk(me, saved, cot, dact, down, gain, start, waits, groups):
    features = cot.shape[1]
    rows = sum(piece.shape[0] for piece in saved)
    rank = down.shape[1]
    pack = jax.ShapeDtypeStruct((rows, features // groups + 2 * rank), jnp.bfloat16)
    outs = [jax.ShapeDtypeStruct((rows, features), jnp.bfloat16)] + [pack] * groups
    got = pl.pallas_call(
        functools.partial(chunk_kernel, start, len(saved), groups),
        out_shape=outs,
        in_specs=[SMEM] + [VMEM] * (4 + len(saved)) + [ANY] * len(waits),
        out_specs=[VMEM] * len(outs),
        scratch_shapes=[pltpu.VMEM((rows, features), jnp.bfloat16)] * 2,
        compiler_params=PARAMS,
    )(me, cot, dact, down, gain, *saved, *waits)
    return got[0], got[1:]


def gather_rows(start, packs, cots, every, held):
    rows = packs[0].shape[0]
    for k, (pack, part) in enumerate(zip(packs, cots)):
        every[pl.ds(k * rows, rows), :] = pack[...]
        held[pl.ds(k * rows, rows), :] = part[pl.ds(start, rows), :]


def sum_kernel(start, groups, *refs):
    packs, cots = refs[:groups], refs[groups : 2 * groups]
    down_ref, up_ref, every, held = refs[-4:]
    width, rank = down_ref.shape
    gather_rows(start, packs, cots, every, held)
    down_ref[...] = rows_dot(every[:, :width], every[:, width : width + rank])
    up_ref[...] = rows_dot(every[:, width + rank :], held[...])


def final_kernel(start, groups, *refs):
    packs, cots = refs[:groups], refs[groups : 2 * groups]
    old_down, old_up, first, last = refs[2 * groups : 2 * groups + 4]
    before_ref, down_ref, up_ref, every, held, down, up, done = refs[2 * groups + 4 :]
    width, rank = down.shape
    rows = first.shape[0]
    copies = [
        pltpu.make_async_copy(first, before_ref.at[pl.ds(0, rows)], done.at[0]),
        pltpu.make_async_copy(last, before_ref.at[pl.ds(rows, last.shape[0])], done.at[1]),
        pltpu.make_async_copy(down, down_ref, done.at[2]),
        pltpu.make_async_copy(up, up_ref, done.at[3]),
    ]
    copies[0].start()
    copies[1].start()
    gather_rows(start, packs, cots, every, held)
    down[...] = old_down[...] + rows_dot(every[:, :width], every[:, width : width + rank])
    copies[2].start()
    up[...] = old_up[...] + rows_dot(every[:, width + rank :], held[...])
    copies[3].start()
    for copy in copies:
        copy.wait()


def gathered(packs, cots):
    depth = len(packs) * packs[0].shape[0]
    return [
        pltpu.VMEM((depth, packs[0].shape[1]), jnp.bfloat16),
        pltpu.VMEM((depth, cots[0].shape[1]), jnp.bfloat16),
    ]


def run_sum(start, packs, cots, waits, rank):
    groups, width = len(cots), cots[0].shape[1]
    return pl.pallas_call(
        functools.partial(sum_kernel, start, groups),
        out_shape=[
            jax.ShapeDtypeStruct((width, rank), jnp.float32),
            jax.ShapeDtypeStruct((rank, width), jnp.float32),
        ],
        in_specs=[VMEM] * (2 * groups) + [ANY] * len(waits),
        out_specs=[VMEM] * 2,
        scratch_shapes=gathered(packs, cots),
        compiler_params=PARAMS,
    )(*packs, *cots, *waits)


def run_final(start, packs, cots, partial, first, last):
    groups = len(cots)
    down, up = [jax.ShapeDtypeStruct(value.shape, jnp.float32) for value in partial]
    before = jax.ShapeDtypeStruct((first.shape[0] + last.shape[0], first.shape[1]), jnp.bfloat16)
    return pl.pallas_call(
        functools.partial(final_kernel, start, groups),
        out_shape=[before, down, up],
        in_specs=[VMEM] * (2 * groups + 4),
        out_specs=[ANY] * 3,
        scratch_shapes=gathered(packs, cots)
        + [
            pltpu.VMEM(down.shape, jnp.float32),
            pltpu.VMEM(up.shape, jnp.float32),
            pltpu.SemaphoreType.DMA((4,)),
        ],
        compiler_params=PARAMS,
    )(*packs, *cots, *partial, first, last)


def per_device(stash_held, grad_in, w_down, w_up, gain):
    sections = lax.axis_size("pipe")
    groups = lax.axis_size("dp")
    me = lax.axis_index("dp")
    stash, cot, down, upper = stash_held[0], grad_in[0], w_down[0], w_up[0]
    tokens, features = cot.shape
    rank = down.shape[1]
    width = features // groups
    sizes = [tokens * share // sum(SHARES) for share in SHARES]
    spans = [(sum(sizes[:i]), size) for i, size in enumerate(sizes)]

    def held(value):
        return exchanged(value, "pipe", sections // 2)

    arrivals = [held(stash[start : start + rows]) for start, rows in spans[:2]]
    cot_all = []
    for k in range(groups):
        part = lax.dynamic_slice_in_dim(cot, (me ^ k) * width, width, axis=1)
        cot_all.append(exchanged(part, "dp", k) if k else part)
    dact = last_dot(cot, upper)
    index = jnp.reshape(me.astype(jnp.int32), (1,))

    coming = rows_after(stash, *spans[2], [arrivals[1]])
    arrivals.append(held(coming))

    def swapped(packs):
        return [exchanged(pack, "dp", k) if k else pack for k, pack in enumerate(packs)]

    late = spans[2][0]
    dx, pack = run_chunk(
        index, arrivals[:2], cot, dact, down, gain, 0, cot_all[1:] + [coming], groups
    )
    first = to_previous(dx, "pipe")
    packs = swapped(pack)
    dx, pack = run_chunk(index, arrivals[2:], cot, dact, down, gain, late, packs[1:], groups)
    last = to_previous(dx, "pipe")
    partial = run_sum(0, packs, cot_all, [pack[0]], rank)
    before, down_grad, up_grad = run_final(late, swapped(pack), cot_all, partial, first, last)
    return (before[None], down_grad[None], up_grad[None])


def solution(mesh):
    in_specs = (
        P("pipe", "dp", None),
        P("pipe", "dp", None),
        P("pipe", None, None),
        P("pipe", None, None),
        P("pipe", None),
    )
    out_specs = (P("pipe", "dp", None), P("pipe", "dp", None), P("pipe", None, "dp"))
    return jax.shard_map(
        per_device, mesh=mesh, in_specs=in_specs, out_specs=out_specs, check_vma=False
    )
```

```python
import functools
import math
import jax
import jax.numpy as jnp
from jax import lax
from jax.experimental import pallas as pl
from jax.experimental.pallas import tpu as pltpu
from jax.sharding import PartitionSpec as P

SHARES = (3, 2, 3)
LANES = 512
VMEM = pl.BlockSpec(memory_space=pltpu.VMEM)
SMEM = pl.BlockSpec(memory_space=pltpu.SMEM)
ANY = pl.BlockSpec(memory_space=pl.ANY)
PARAMS = pltpu.CompilerParams(vmem_limit_bytes=16 * 1024 * 1024)
SUMCOST = pl.CostEstimate(flops=30 * 10**8, bytes_accessed=10**6, transcendentals=0)
COSTS = [pl.CostEstimate(flops=f, bytes_accessed=1, transcendentals=0) for f in (0 * 10**8, 0 * 10**8, 80 * 10**8)]
SMALL = pltpu.CompilerParams(vmem_limit_bytes=4 * 1024 * 1024)


def exchanged(x, axis, mask):
    return lax.ppermute(x, axis, [(i, i ^ mask) for i in range(lax.axis_size(axis))])


def to_previous(x, axis):
    return lax.ppermute(x, axis, [(i, i - 1) for i in range(1, lax.axis_size(axis))])


def rows_dot(a, b):
    return lax.dot_general(a, b, (((0,), (0,)), ((), ())), preferred_element_type=jnp.float32)


def last_dot(a, b):
    return lax.dot_general(a, b, (((1,), (1,)), ((), ())), preferred_element_type=jnp.float32)


def gelu_and_slope(x):
    c = math.sqrt(2.0 / math.pi)
    th = jnp.tanh(c * (x + 0.044715 * (x * x * x)))
    slope = 0.5 * (1.0 + th) + 0.5 * x * (1.0 - th * th) * (c * (1.0 + 3.0 * 0.044715 * (x * x)))
    return 0.5 * x * (1.0 + th), slope


def copy_kernel(start, stash_ref, *refs):
    out_ref, done = refs[-2:]
    copy = pltpu.make_async_copy(stash_ref.at[pl.ds(start, out_ref.shape[0])], out_ref, done)
    copy.start()
    copy.wait()


def rows_after(stash, start, rows, waits):
    return pl.pallas_call(
        functools.partial(copy_kernel, start),
        out_shape=jax.ShapeDtypeStruct((rows, stash.shape[1]), stash.dtype),
        in_specs=[ANY] * (1 + len(waits)),
        out_specs=VMEM,
        scratch_shapes=[pltpu.SemaphoreType.DMA],
        compiler_params=SMALL,
    )(stash, *waits)


def chunk_kernel(start, joins, waits, me_ref, saved_ref, cot_ref, dact_ref, down_ref, gain_ref, *refs):
    outs = refs[joins + waits :]
    dx_ref, pack_refs, normed_ref = outs[0], outs[1:-1], outs[-1]
    groups = len(pack_refs)
    rows, features = saved_ref.shape
    ahead = dx_ref.shape[0] - rows
    at = 0
    for part in refs[:joins]:
        dx_ref[pl.ds(at, part.shape[0]), :] = part[...]
        at += part.shape[0]
    width = features // groups
    rank = down_ref.shape[1]
    lanes = [pl.ds(f, LANES) for f in range(0, features, LANES)]
    total = jnp.zeros((rows, 1), jnp.float32)
    for at in lanes:
        xf = saved_ref[:, at].astype(jnp.float32)
        total += jnp.sum(xf * xf, axis=1, keepdims=True)
    inverse = 1.0 / jnp.sqrt(total / features + 1e-05)
    for at in lanes:
        unit = saved_ref[:, at].astype(jnp.float32) * inverse
        normed_ref[:, at] = (unit * gain_ref[:, at]).astype(jnp.bfloat16)
    pre = jnp.dot(normed_ref[...], down_ref[...], preferred_element_type=jnp.float32)
    act, slope = gelu_and_slope(pre)
    act = act.astype(jnp.bfloat16)
    dpre = (dact_ref[pl.ds(start, rows), :] * slope).astype(jnp.bfloat16)
    inner = jnp.sum(dpre.astype(jnp.float32) * pre, axis=1, keepdims=True) / features
    for k in range(groups):
        at = pl.ds(pl.multiple_of((me_ref[0] ^ k) * width, 128), width)
        pack_refs[k][:, :width] = normed_ref[:, at]
        pack_refs[k][:, width : width + rank] = dpre
        pack_refs[k][:, width + rank :] = act
    pull = inner * inverse
    for at in lanes:
        dnorm = last_dot(dpre, down_ref[at, :]) * gain_ref[:, at]
        xf = saved_ref[:, at].astype(jnp.float32)
        held = cot_ref[pl.ds(start, rows), at].astype(jnp.float32)
        dx_ref[pl.ds(ahead, rows), at] = (held + (dnorm - xf * pull) * inverse).astype(jnp.bfloat16)


def run_chunk(me, saved, cot, dact, down, gain, start, joins, waits, groups, cost):
    rows, features = saved.shape
    rank = down.shape[1]
    pack = jax.ShapeDtypeStruct((rows, features // groups + 2 * rank), jnp.bfloat16)
    ahead = sum(part.shape[0] for part in joins)
    outs = [jax.ShapeDtypeStruct((ahead + rows, features), jnp.bfloat16)] + [pack] * groups
    got = pl.pallas_call(
        functools.partial(chunk_kernel, start, len(joins), len(waits)),
        out_shape=outs,
        in_specs=[SMEM] + [VMEM] * (5 + len(joins)) + [ANY] * len(waits),
        out_specs=[VMEM] * len(outs),
        scratch_shapes=[pltpu.VMEM((rows, features), jnp.bfloat16)],
        cost_estimate=cost,
        compiler_params=PARAMS,
    )(me, saved, cot, dact, down, gain, *joins, *waits)
    return got[0], got[1:]


def gather_rows(groups, spans, packs, cots, every, held):
    at = 0
    for k in range(groups):
        for j, (start, rows) in enumerate(spans):
            every[pl.ds(at, rows), :] = packs[k * len(spans) + j][...]
            held[pl.ds(at, rows), :] = cots[k][pl.ds(start, rows), :]
            at += rows


def sum_kernel(groups, spans, *refs):
    count = groups * len(spans)
    packs, cots = refs[:count], refs[count : count + groups]
    down_ref, up_ref, every, held = refs[-4:]
    width, rank = down_ref.shape
    gather_rows(groups, spans, packs, cots, every, held)
    down_ref[...] = rows_dot(every[:, :width], every[:, width : width + rank])
    up_ref[...] = rows_dot(every[:, width + rank :], held[...])


def final_kernel(groups, spans, *refs):
    packs, cots = refs[:groups], refs[groups : 2 * groups]
    old_down, old_up, first = refs[2 * groups : 2 * groups + 3]
    before_ref, down_ref, up_ref, every, held, down, up, done = refs[2 * groups + 3 :]
    width, rank = down.shape
    copies = [
        pltpu.make_async_copy(first, before_ref.at[pl.ds(0, first.shape[0])], done.at[0]),
        pltpu.make_async_copy(down, down_ref, done.at[1]),
        pltpu.make_async_copy(up, up_ref, done.at[2]),
    ]
    copies[0].start()
    gather_rows(groups, spans, packs, cots, every, held)
    down[...] = old_down[...] + rows_dot(every[:, :width], every[:, width : width + rank])
    copies[1].start()
    up[...] = old_up[...] + rows_dot(every[:, width + rank :], held[...])
    copies[2].start()
    for copy in copies:
        copy.wait()


def join_kernel(start, before_ref, last, out_ref, done):
    copy = pltpu.make_async_copy(last, out_ref.at[pl.ds(start, last.shape[0])], done)
    copy.start()
    copy.wait()


def run_join(before, last):
    return pl.pallas_call(
        functools.partial(join_kernel, before.shape[0] - last.shape[0]),
        out_shape=jax.ShapeDtypeStruct(before.shape, before.dtype),
        in_specs=[ANY, VMEM],
        out_specs=ANY,
        scratch_shapes=[pltpu.SemaphoreType.DMA],
        input_output_aliases={0: 0},
        compiler_params=SMALL,
    )(before, last)


def operands(packs, cots, spans):
    groups = len(cots)
    width = cots[0].shape[1]
    depth = groups * sum(rows for _, rows in spans)
    args = [packs[j][k] for k in range(groups) for j in range(len(spans))] + list(cots)
    scratch = [
        pltpu.VMEM((depth, packs[0][0].shape[1]), jnp.bfloat16),
        pltpu.VMEM((depth, width), jnp.bfloat16),
    ]
    return groups, width, args, scratch


def run_sum(packs, cots, spans, waits, rank):
    groups, width, args, scratch = operands(packs, cots, spans)
    return pl.pallas_call(
        functools.partial(sum_kernel, groups, spans),
        out_shape=[
            jax.ShapeDtypeStruct((width, rank), jnp.float32),
            jax.ShapeDtypeStruct((rank, width), jnp.float32),
        ],
        in_specs=[VMEM] * len(args) + [ANY] * len(waits),
        out_specs=[VMEM] * 2,
        scratch_shapes=scratch,
        compiler_params=PARAMS,
    )(*args, *waits)


def run_final(packs, cots, spans, partial, first, tokens):
    groups, width, args, scratch = operands(packs, cots, spans)
    down, up = [jax.ShapeDtypeStruct(value.shape, jnp.float32) for value in partial]
    scratch += [
        pltpu.VMEM(down.shape, jnp.float32),
        pltpu.VMEM(up.shape, jnp.float32),
        pltpu.SemaphoreType.DMA((3,)),
    ]
    return pl.pallas_call(
        functools.partial(final_kernel, groups, spans),
        out_shape=[jax.ShapeDtypeStruct((tokens, first.shape[1]), first.dtype), down, up],
        in_specs=[VMEM] * (len(args) + 3),
        out_specs=[ANY] * 3,
        scratch_shapes=scratch,
        compiler_params=PARAMS,
        cost_estimate=SUMCOST,
    )(*args, *partial, first)


def per_device(stash_held, grad_in, w_down, w_up, gain):
    sections = lax.axis_size("pipe")
    groups = lax.axis_size("dp")
    me = lax.axis_index("dp")
    stash, cot, down, upper = stash_held[0], grad_in[0], w_down[0], w_up[0]
    tokens, features = cot.shape
    rank = down.shape[1]
    width = features // groups
    sizes = [tokens * share // sum(SHARES) for share in SHARES]
    spans = [(sum(sizes[:i]), size) for i, size in enumerate(sizes)]
    chunks = len(spans)

    def held(value):
        return exchanged(value, "pipe", sections // 2)

    arrivals = [held(stash[start : start + rows]) for start, rows in spans[:2]]
    cot_all = []
    for k in range(groups):
        part = lax.dynamic_slice_in_dim(cot, (me ^ k) * width, width, axis=1)
        cot_all.append(exchanged(part, "dp", k) if k else part)
    dact = last_dot(cot, upper)
    index = jnp.reshape(me.astype(jnp.int32), (1,))

    parts, packs, waits = [], [], cot_all[1:]
    for i, (start, rows) in enumerate(spans):
        if i + 2 < chunks:
            coming = rows_after(stash, *spans[i + 2], [arrivals[i]] + waits * (i > 0))
            arrivals.append(held(coming))
            waits = waits + [coming]
        joins = parts if i == chunks - 2 else []
        dx, pack = run_chunk(index, arrivals[i], cot, dact, down, gain, start, joins, waits, groups, COSTS[i])
        packs.append([exchanged(pack[k], "dp", k) if k else pack[k] for k in range(groups)])
        parts.append(dx)
        waits = packs[-1][1:]
    first, last = [to_previous(dx, "pipe") for dx in parts[-2:]]
    partial = run_sum(packs[:-1], cot_all, spans[:-1], [pack[0]], rank)
    before, down_grad, up_grad = run_final(
        packs[-1:], cot_all, spans[-1:], partial, first, tokens
    )
    before = run_join(before, last)
    return (before[None], down_grad[None], up_grad[None])


def solution(mesh):
    in_specs = (
        P("pipe", "dp", None),
        P("pipe", "dp", None),
        P("pipe", None, None),
        P("pipe", None, None),
        P("pipe", None),
    )
    out_specs = (P("pipe", "dp", None), P("pipe", "dp", None), P("pipe", None, "dp"))
    return jax.shard_map(
        per_device, mesh=mesh, in_specs=in_specs, out_specs=out_specs, check_vma=False
    )
```

```python
import functools
import math
import jax
import jax.numpy as jnp
from jax import lax
from jax.experimental import pallas as pl
from jax.experimental.pallas import tpu as pltpu
from jax.sharding import PartitionSpec as P

SHARES = (1, 3, 1, 3)
LANES = 512
VMEM = pl.BlockSpec(memory_space=pltpu.VMEM)
SMEM = pl.BlockSpec(memory_space=pltpu.SMEM)
ANY = pl.BlockSpec(memory_space=pl.ANY)
PARAMS = pltpu.CompilerParams(vmem_limit_bytes=16 * 1024 * 1024)
SUMCOST = pl.CostEstimate(flops=30 * 10**8, bytes_accessed=10**6, transcendentals=0)
COSTS = [pl.CostEstimate(flops=f, bytes_accessed=1, transcendentals=0) for f in (0 * 10**8, 0 * 10**8, 60 * 10**8, 90 * 10**8)]
SMALL = pltpu.CompilerParams(vmem_limit_bytes=4 * 1024 * 1024)


def exchanged(x, axis, mask):
    return lax.ppermute(x, axis, [(i, i ^ mask) for i in range(lax.axis_size(axis))])


def to_previous(x, axis):
    return lax.ppermute(x, axis, [(i, i - 1) for i in range(1, lax.axis_size(axis))])


def rows_dot(a, b):
    return lax.dot_general(a, b, (((0,), (0,)), ((), ())), preferred_element_type=jnp.float32)


def last_dot(a, b):
    return lax.dot_general(a, b, (((1,), (1,)), ((), ())), preferred_element_type=jnp.float32)


def gelu_and_slope(x):
    c = math.sqrt(2.0 / math.pi)
    th = jnp.tanh(c * (x + 0.044715 * (x * x * x)))
    slope = 0.5 * (1.0 + th) + 0.5 * x * (1.0 - th * th) * (c * (1.0 + 3.0 * 0.044715 * (x * x)))
    return 0.5 * x * (1.0 + th), slope


def copy_kernel(start, stash_ref, *refs):
    out_ref, done = refs[-2:]
    copy = pltpu.make_async_copy(stash_ref.at[pl.ds(start, out_ref.shape[0])], out_ref, done)
    copy.start()
    copy.wait()


def rows_after(stash, start, rows, waits):
    return pl.pallas_call(
        functools.partial(copy_kernel, start),
        out_shape=jax.ShapeDtypeStruct((rows, stash.shape[1]), stash.dtype),
        in_specs=[ANY] * (1 + len(waits)),
        out_specs=VMEM,
        scratch_shapes=[pltpu.SemaphoreType.DMA],
        compiler_params=SMALL,
    )(stash, *waits)


def chunk_kernel(start, joins, waits, me_ref, saved_ref, cot_ref, dact_ref, down_ref, gain_ref, *refs):
    outs = refs[joins + waits :]
    dx_ref, pack_refs, normed_ref = outs[0], outs[1:-1], outs[-1]
    groups = len(pack_refs)
    rows, features = saved_ref.shape
    ahead = dx_ref.shape[0] - rows
    at = 0
    for part in refs[:joins]:
        dx_ref[pl.ds(at, part.shape[0]), :] = part[...]
        at += part.shape[0]
    width = features // groups
    rank = down_ref.shape[1]
    lanes = [pl.ds(f, LANES) for f in range(0, features, LANES)]
    total = jnp.zeros((rows, 1), jnp.float32)
    for at in lanes:
        xf = saved_ref[:, at].astype(jnp.float32)
        total += jnp.sum(xf * xf, axis=1, keepdims=True)
    inverse = 1.0 / jnp.sqrt(total / features + 1e-05)
    for at in lanes:
        unit = saved_ref[:, at].astype(jnp.float32) * inverse
        normed_ref[:, at] = (unit * gain_ref[:, at]).astype(jnp.bfloat16)
    pre = jnp.dot(normed_ref[...], down_ref[...], preferred_element_type=jnp.float32)
    act, slope = gelu_and_slope(pre)
    act = act.astype(jnp.bfloat16)
    dpre = (dact_ref[pl.ds(start, rows), :] * slope).astype(jnp.bfloat16)
    inner = jnp.sum(dpre.astype(jnp.float32) * pre, axis=1, keepdims=True) / features
    for k in range(groups):
        at = pl.ds(pl.multiple_of((me_ref[0] ^ k) * width, 128), width)
        pack_refs[k][:, :width] = normed_ref[:, at]
        pack_refs[k][:, width : width + rank] = dpre
        pack_refs[k][:, width + rank :] = act
    pull = inner * inverse
    for at in lanes:
        dnorm = last_dot(dpre, down_ref[at, :]) * gain_ref[:, at]
        xf = saved_ref[:, at].astype(jnp.float32)
        held = cot_ref[pl.ds(start, rows), at].astype(jnp.float32)
        dx_ref[pl.ds(ahead, rows), at] = (held + (dnorm - xf * pull) * inverse).astype(jnp.bfloat16)


def run_chunk(me, saved, cot, dact, down, gain, start, joins, waits, groups, cost):
    rows, features = saved.shape
    rank = down.shape[1]
    pack = jax.ShapeDtypeStruct((rows, features // groups + 2 * rank), jnp.bfloat16)
    ahead = sum(part.shape[0] for part in joins)
    outs = [jax.ShapeDtypeStruct((ahead + rows, features), jnp.bfloat16)] + [pack] * groups
    got = pl.pallas_call(
        functools.partial(chunk_kernel, start, len(joins), len(waits)),
        out_shape=outs,
        in_specs=[SMEM] + [VMEM] * (5 + len(joins)) + [ANY] * len(waits),
        out_specs=[VMEM] * len(outs),
        scratch_shapes=[pltpu.VMEM((rows, features), jnp.bfloat16)],
        cost_estimate=cost,
        compiler_params=PARAMS,
    )(me, saved, cot, dact, down, gain, *joins, *waits)
    return got[0], got[1:]


def gather_rows(groups, spans, packs, cots, every, held):
    at = 0
    for k in range(groups):
        for j, (start, rows) in enumerate(spans):
            every[pl.ds(at, rows), :] = packs[k * len(spans) + j][...]
            held[pl.ds(at, rows), :] = cots[k][pl.ds(start, rows), :]
            at += rows


def sum_kernel(groups, spans, *refs):
    count = groups * len(spans)
    packs, cots = refs[:count], refs[count : count + groups]
    down_ref, up_ref, every, held = refs[-4:]
    width, rank = down_ref.shape
    gather_rows(groups, spans, packs, cots, every, held)
    down_ref[...] = rows_dot(every[:, :width], every[:, width : width + rank])
    up_ref[...] = rows_dot(every[:, width + rank :], held[...])


def final_kernel(groups, spans, *refs):
    packs, cots = refs[:groups], refs[groups : 2 * groups]
    old_down, old_up, first = refs[2 * groups : 2 * groups + 3]
    before_ref, down_ref, up_ref, every, held, down, up, done = refs[2 * groups + 3 :]
    width, rank = down.shape
    copies = [
        pltpu.make_async_copy(first, before_ref.at[pl.ds(0, first.shape[0])], done.at[0]),
        pltpu.make_async_copy(down, down_ref, done.at[1]),
        pltpu.make_async_copy(up, up_ref, done.at[2]),
    ]
    copies[0].start()
    gather_rows(groups, spans, packs, cots, every, held)
    down[...] = old_down[...] + rows_dot(every[:, :width], every[:, width : width + rank])
    copies[1].start()
    up[...] = old_up[...] + rows_dot(every[:, width + rank :], held[...])
    copies[2].start()
    for copy in copies:
        copy.wait()


def join_kernel(start, before_ref, last, out_ref, done):
    copy = pltpu.make_async_copy(last, out_ref.at[pl.ds(start, last.shape[0])], done)
    copy.start()
    copy.wait()


def run_join(before, last):
    return pl.pallas_call(
        functools.partial(join_kernel, before.shape[0] - last.shape[0]),
        out_shape=jax.ShapeDtypeStruct(before.shape, before.dtype),
        in_specs=[ANY, VMEM],
        out_specs=ANY,
        scratch_shapes=[pltpu.SemaphoreType.DMA],
        input_output_aliases={0: 0},
        compiler_params=SMALL,
    )(before, last)


def operands(packs, cots, spans):
    groups = len(cots)
    width = cots[0].shape[1]
    depth = groups * sum(rows for _, rows in spans)
    args = [packs[j][k] for k in range(groups) for j in range(len(spans))] + list(cots)
    scratch = [
        pltpu.VMEM((depth, packs[0][0].shape[1]), jnp.bfloat16),
        pltpu.VMEM((depth, width), jnp.bfloat16),
    ]
    return groups, width, args, scratch


def run_sum(packs, cots, spans, waits, rank):
    groups, width, args, scratch = operands(packs, cots, spans)
    return pl.pallas_call(
        functools.partial(sum_kernel, groups, spans),
        out_shape=[
            jax.ShapeDtypeStruct((width, rank), jnp.float32),
            jax.ShapeDtypeStruct((rank, width), jnp.float32),
        ],
        in_specs=[VMEM] * len(args) + [ANY] * len(waits),
        out_specs=[VMEM] * 2,
        scratch_shapes=scratch,
        compiler_params=PARAMS,
    )(*args, *waits)


def run_final(packs, cots, spans, partial, first, tokens):
    groups, width, args, scratch = operands(packs, cots, spans)
    down, up = [jax.ShapeDtypeStruct(value.shape, jnp.float32) for value in partial]
    scratch += [
        pltpu.VMEM(down.shape, jnp.float32),
        pltpu.VMEM(up.shape, jnp.float32),
        pltpu.SemaphoreType.DMA((3,)),
    ]
    return pl.pallas_call(
        functools.partial(final_kernel, groups, spans),
        out_shape=[jax.ShapeDtypeStruct((tokens, first.shape[1]), first.dtype), down, up],
        in_specs=[VMEM] * (len(args) + 3),
        out_specs=[ANY] * 3,
        scratch_shapes=scratch,
        compiler_params=PARAMS,
        cost_estimate=SUMCOST,
    )(*args, *partial, first)


def per_device(stash_held, grad_in, w_down, w_up, gain):
    sections = lax.axis_size("pipe")
    groups = lax.axis_size("dp")
    me = lax.axis_index("dp")
    stash, cot, down, upper = stash_held[0], grad_in[0], w_down[0], w_up[0]
    tokens, features = cot.shape
    rank = down.shape[1]
    width = features // groups
    sizes = [tokens * share // sum(SHARES) for share in SHARES]
    spans = [(sum(sizes[:i]), size) for i, size in enumerate(sizes)]
    chunks = len(spans)

    def held(value):
        return exchanged(value, "pipe", sections // 2)

    arrivals = [held(stash[start : start + rows]) for start, rows in spans[:2]]
    cot_all = []
    for k in range(groups):
        part = lax.dynamic_slice_in_dim(cot, (me ^ k) * width, width, axis=1)
        cot_all.append(exchanged(part, "dp", k) if k else part)
    dact = last_dot(cot, upper)
    index = jnp.reshape(me.astype(jnp.int32), (1,))

    parts, packs, waits = [], [], cot_all[1:]
    for i, (start, rows) in enumerate(spans):
        if i + 2 < chunks:
            coming = rows_after(stash, *spans[i + 2], [arrivals[i]] + waits * (i > 0))
            arrivals.append(held(coming))
            waits = waits + [coming]
        joins = parts if i == chunks - 2 else []
        dx, pack = run_chunk(index, arrivals[i], cot, dact, down, gain, start, joins, waits, groups, COSTS[i])
        packs.append([exchanged(pack[k], "dp", k) if k else pack[k] for k in range(groups)])
        parts.append(dx)
        waits = packs[-1][1:]
    first, last = [to_previous(dx, "pipe") for dx in parts[-2:]]
    partial = run_sum(packs[:-1], cot_all, spans[:-1], [pack[0]], rank)
    before, down_grad, up_grad = run_final(
        packs[-1:], cot_all, spans[-1:], partial, first, tokens
    )
    before = run_join(before, last)
    return (before[None], down_grad[None], up_grad[None])


def solution(mesh):
    in_specs = (
        P("pipe", "dp", None),
        P("pipe", "dp", None),
        P("pipe", None, None),
        P("pipe", None, None),
        P("pipe", None),
    )
    out_specs = (P("pipe", "dp", None), P("pipe", "dp", None), P("pipe", None, "dp"))
    return jax.shard_map(
        per_device, mesh=mesh, in_specs=in_specs, out_specs=out_specs, check_vma=False
    )
```

```python
import functools
import math
import jax
import jax.numpy as jnp
from jax import lax
from jax.experimental import pallas as pl
from jax.experimental.pallas import tpu as pltpu
from jax.sharding import PartitionSpec as P

SHARES = (1, 3, 1, 3)
LANES = 512
VMEM = pl.BlockSpec(memory_space=pltpu.VMEM)
SMEM = pl.BlockSpec(memory_space=pltpu.SMEM)
ANY = pl.BlockSpec(memory_space=pl.ANY)
PARAMS = pltpu.CompilerParams(vmem_limit_bytes=16 * 1024 * 1024)
SUMCOST = pl.CostEstimate(flops=30 * 10**8, bytes_accessed=10**6, transcendentals=0)
COSTS = [pl.CostEstimate(flops=f, bytes_accessed=1, transcendentals=0) for f in (0 * 10**8, 0 * 10**8, 60 * 10**8, 90 * 10**8)]
SMALL = pltpu.CompilerParams(vmem_limit_bytes=4 * 1024 * 1024)


def exchanged(x, axis, mask):
    return lax.ppermute(x, axis, [(i, i ^ mask) for i in range(lax.axis_size(axis))])


def to_previous(x, axis):
    return lax.ppermute(x, axis, [(i, i - 1) for i in range(1, lax.axis_size(axis))])


def rows_dot(a, b):
    return lax.dot_general(a, b, (((0,), (0,)), ((), ())), preferred_element_type=jnp.float32)


def last_dot(a, b):
    return lax.dot_general(a, b, (((1,), (1,)), ((), ())), preferred_element_type=jnp.float32)


def gelu_and_slope(x):
    c = math.sqrt(2.0 / math.pi)
    th = jnp.tanh(c * (x + 0.044715 * (x * x * x)))
    slope = 0.5 * (1.0 + th) + 0.5 * x * (1.0 - th * th) * (c * (1.0 + 3.0 * 0.044715 * (x * x)))
    return 0.5 * x * (1.0 + th), slope


def copy_kernel(start, stash_ref, *refs):
    out_ref, done = refs[-2:]
    copy = pltpu.make_async_copy(stash_ref.at[pl.ds(start, out_ref.shape[0])], out_ref, done)
    copy.start()
    copy.wait()


def rows_after(stash, start, rows, waits):
    return pl.pallas_call(
        functools.partial(copy_kernel, start),
        out_shape=jax.ShapeDtypeStruct((rows, stash.shape[1]), stash.dtype),
        in_specs=[ANY] * (1 + len(waits)),
        out_specs=VMEM,
        scratch_shapes=[pltpu.SemaphoreType.DMA],
        compiler_params=SMALL,
    )(stash, *waits)


def chunk_kernel(start, joins, waits, me_ref, saved_ref, cot_ref, dact_ref, down_ref, gain_ref, *refs):
    outs = refs[joins + waits :]
    dx_ref, pack_refs, normed_ref = outs[0], outs[1:-1], outs[-1]
    groups = len(pack_refs)
    rows, features = saved_ref.shape
    ahead = dx_ref.shape[0] - rows
    at = 0
    for part in refs[:joins]:
        dx_ref[pl.ds(at, part.shape[0]), :] = part[...]
        at += part.shape[0]
    width = features // groups
    rank = down_ref.shape[1]
    lanes = [pl.ds(f, LANES) for f in range(0, features, LANES)]
    total = jnp.zeros((rows, 1), jnp.float32)
    for at in lanes:
        xf = saved_ref[:, at].astype(jnp.float32)
        total += jnp.sum(xf * xf, axis=1, keepdims=True)
    inverse = 1.0 / jnp.sqrt(total / features + 1e-05)
    for at in lanes:
        unit = saved_ref[:, at].astype(jnp.float32) * inverse
        normed_ref[:, at] = (unit * gain_ref[:, at]).astype(jnp.bfloat16)
    pre = jnp.dot(normed_ref[...], down_ref[...], preferred_element_type=jnp.float32)
    act, slope = gelu_and_slope(pre)
    act = act.astype(jnp.bfloat16)
    dpre = (dact_ref[pl.ds(start, rows), :] * slope).astype(jnp.bfloat16)
    inner = jnp.sum(dpre.astype(jnp.float32) * pre, axis=1, keepdims=True) / features
    for k in range(groups):
        at = pl.ds(pl.multiple_of((me_ref[0] ^ k) * width, 128), width)
        pack_refs[k][:, :width] = normed_ref[:, at]
        pack_refs[k][:, width : width + rank] = dpre
        pack_refs[k][:, width + rank :] = act
    pull = inner * inverse
    for at in lanes:
        dnorm = last_dot(dpre, down_ref[at, :]) * gain_ref[:, at]
        xf = saved_ref[:, at].astype(jnp.float32)
        held = cot_ref[pl.ds(start, rows), at].astype(jnp.float32)
        dx_ref[pl.ds(ahead, rows), at] = (held + (dnorm - xf * pull) * inverse).astype(jnp.bfloat16)


def run_chunk(me, saved, cot, dact, down, gain, start, joins, waits, groups, cost):
    rows, features = saved.shape
    rank = down.shape[1]
    pack = jax.ShapeDtypeStruct((rows, features // groups + 2 * rank), jnp.bfloat16)
    ahead = sum(part.shape[0] for part in joins)
    outs = [jax.ShapeDtypeStruct((ahead + rows, features), jnp.bfloat16)] + [pack] * groups
    got = pl.pallas_call(
        functools.partial(chunk_kernel, start, len(joins), len(waits)),
        out_shape=outs,
        in_specs=[SMEM] + [VMEM] * (5 + len(joins)) + [ANY] * len(waits),
        out_specs=[VMEM] * len(outs),
        scratch_shapes=[pltpu.VMEM((rows, features), jnp.bfloat16)],
        cost_estimate=cost,
        compiler_params=PARAMS,
    )(me, saved, cot, dact, down, gain, *joins, *waits)
    return got[0], got[1:]


def gather_rows(groups, spans, packs, cots, every, held):
    at = 0
    for k in range(groups):
        for j, (start, rows) in enumerate(spans):
            every[pl.ds(at, rows), :] = packs[k * len(spans) + j][...]
            held[pl.ds(at, rows), :] = cots[k][pl.ds(start, rows), :]
            at += rows


def sum_kernel(groups, spans, *refs):
    count = groups * len(spans)
    packs, cots = refs[:count], refs[count : count + groups]
    down_ref, up_ref, every, held = refs[-4:]
    width, rank = down_ref.shape
    gather_rows(groups, spans, packs, cots, every, held)
    own = refs[count + groups]
    rows = own.shape[0]
    rest = pl.ds(every.shape[0] - rows, rows)
    every[rest, :] = own[...]
    held[rest, :] = cots[0][pl.ds(cots[0].shape[0] - rows, rows), :]
    down_ref[...] = rows_dot(every[:, :width], every[:, width : width + rank])
    up_ref[...] = rows_dot(every[:, width + rank :], held[...])


def final_kernel(groups, spans, *refs):
    packs, cots = refs[:groups], refs[groups : 2 * groups]
    old_down, old_up, first = refs[2 * groups : 2 * groups + 3]
    before_ref, down_ref, up_ref, every, held, down, up, done = refs[2 * groups + 3 :]
    width, rank = down.shape
    copies = [
        pltpu.make_async_copy(first, before_ref.at[pl.ds(0, first.shape[0])], done.at[0]),
        pltpu.make_async_copy(down, down_ref, done.at[1]),
        pltpu.make_async_copy(up, up_ref, done.at[2]),
    ]
    copies[0].start()
    gather_rows(groups, spans, packs, cots, every, held)
    down[...] = old_down[...] + rows_dot(every[:, :width], every[:, width : width + rank])
    copies[1].start()
    up[...] = old_up[...] + rows_dot(every[:, width + rank :], held[...])
    copies[2].start()
    for copy in copies:
        copy.wait()


def join_kernel(start, before_ref, last, out_ref, done):
    copy = pltpu.make_async_copy(last, out_ref.at[pl.ds(start, last.shape[0])], done)
    copy.start()
    copy.wait()


def run_join(before, last):
    return pl.pallas_call(
        functools.partial(join_kernel, before.shape[0] - last.shape[0]),
        out_shape=jax.ShapeDtypeStruct(before.shape, before.dtype),
        in_specs=[ANY, VMEM],
        out_specs=ANY,
        scratch_shapes=[pltpu.SemaphoreType.DMA],
        input_output_aliases={0: 0},
        compiler_params=SMALL,
    )(before, last)


def operands(packs, cots, spans, more=0):
    groups = len(cots)
    width = cots[0].shape[1]
    depth = groups * sum(rows for _, rows in spans) + more
    args = [packs[j][k] for k in range(groups) for j in range(len(spans))] + list(cots)
    scratch = [
        pltpu.VMEM((depth, packs[0][0].shape[1]), jnp.bfloat16),
        pltpu.VMEM((depth, width), jnp.bfloat16),
    ]
    return groups, width, args, scratch


def run_sum(packs, cots, spans, own, rank):
    groups, width, args, scratch = operands(packs, cots, spans, own.shape[0])
    return pl.pallas_call(
        functools.partial(sum_kernel, groups, spans),
        out_shape=[
            jax.ShapeDtypeStruct((width, rank), jnp.float32),
            jax.ShapeDtypeStruct((rank, width), jnp.float32),
        ],
        in_specs=[VMEM] * (len(args) + 1),
        out_specs=[VMEM] * 2,
        scratch_shapes=scratch,
        compiler_params=PARAMS,
    )(*args, own)


def run_final(packs, cots, spans, partial, first, tokens):
    groups, width, args, scratch = operands(packs, cots, spans)
    down, up = [jax.ShapeDtypeStruct(value.shape, jnp.float32) for value in partial]
    scratch += [
        pltpu.VMEM(down.shape, jnp.float32),
        pltpu.VMEM(up.shape, jnp.float32),
        pltpu.SemaphoreType.DMA((3,)),
    ]
    return pl.pallas_call(
        functools.partial(final_kernel, groups, spans),
        out_shape=[jax.ShapeDtypeStruct((tokens, first.shape[1]), first.dtype), down, up],
        in_specs=[VMEM] * (len(args) + 3),
        out_specs=[ANY] * 3,
        scratch_shapes=scratch,
        compiler_params=PARAMS,
        cost_estimate=SUMCOST,
    )(*args, *partial, first)


def per_device(stash_held, grad_in, w_down, w_up, gain):
    sections = lax.axis_size("pipe")
    groups = lax.axis_size("dp")
    me = lax.axis_index("dp")
    stash, cot, down, upper = stash_held[0], grad_in[0], w_down[0], w_up[0]
    tokens, features = cot.shape
    rank = down.shape[1]
    width = features // groups
    sizes = [tokens * share // sum(SHARES) for share in SHARES]
    spans = [(sum(sizes[:i]), size) for i, size in enumerate(sizes)]
    chunks = len(spans)

    def held(value):
        return exchanged(value, "pipe", sections // 2)

    arrivals = [held(stash[start : start + rows]) for start, rows in spans[:2]]
    cot_all = []
    for k in range(groups):
        part = lax.dynamic_slice_in_dim(cot, (me ^ k) * width, width, axis=1)
        cot_all.append(exchanged(part, "dp", k) if k else part)
    dact = last_dot(cot, upper)
    index = jnp.reshape(me.astype(jnp.int32), (1,))

    parts, packs, waits = [], [], cot_all[1:]
    for i, (start, rows) in enumerate(spans):
        if i + 2 < chunks:
            coming = rows_after(stash, *spans[i + 2], [arrivals[i]] + waits[:1] * (i > 0))
            arrivals.append(held(coming))
            waits = waits + [coming]
        joins = parts if i == chunks - 2 else []
        dx, pack = run_chunk(index, arrivals[i], cot, dact, down, gain, start, joins, waits, groups, COSTS[i])
        packs.append([exchanged(pack[k], "dp", k) if k else pack[k] for k in range(groups)])
        parts.append(dx)
        waits = packs[-1][1:]
    first, last = [to_previous(dx, "pipe") for dx in parts[-2:]]
    partial = run_sum(packs[:-1], cot_all, spans[:-1], pack[0], rank)
    before, down_grad, up_grad = run_final(
        [packs[-1][1:]], cot_all[1:], spans[-1:], partial, first, tokens
    )
    before = run_join(before, last)
    return (before[None], down_grad[None], up_grad[None])


def solution(mesh):
    in_specs = (
        P("pipe", "dp", None),
        P("pipe", "dp", None),
        P("pipe", None, None),
        P("pipe", None, None),
        P("pipe", None),
    )
    out_specs = (P("pipe", "dp", None), P("pipe", "dp", None), P("pipe", None, "dp"))
    return jax.shard_map(
        per_device, mesh=mesh, in_specs=in_specs, out_specs=out_specs, check_vma=False
    )
```

```python
import functools
import math
import jax
import jax.numpy as jnp
from jax import lax
from jax.experimental import pallas as pl
from jax.experimental.pallas import tpu as pltpu
from jax.sharding import PartitionSpec as P

SHARES = (1, 3, 1, 3)
LANES = 512
VMEM = pl.BlockSpec(memory_space=pltpu.VMEM)
SMEM = pl.BlockSpec(memory_space=pltpu.SMEM)
ANY = pl.BlockSpec(memory_space=pl.ANY)
PARAMS = pltpu.CompilerParams(vmem_limit_bytes=16 * 1024 * 1024)
SUMCOST = pl.CostEstimate(flops=30 * 10**8, bytes_accessed=10**6, transcendentals=0)
COSTS = [pl.CostEstimate(flops=f, bytes_accessed=1, transcendentals=0) for f in (0 * 10**8, 0 * 10**8, 60 * 10**8, 90 * 10**8)]
SMALL = pltpu.CompilerParams(vmem_limit_bytes=4 * 1024 * 1024)


def exchanged(x, axis, mask):
    return lax.ppermute(x, axis, [(i, i ^ mask) for i in range(lax.axis_size(axis))])


def to_previous(x, axis):
    return lax.ppermute(x, axis, [(i, i - 1) for i in range(1, lax.axis_size(axis))])


def rows_dot(a, b):
    return lax.dot_general(a, b, (((0,), (0,)), ((), ())), preferred_element_type=jnp.float32)


def last_dot(a, b):
    return lax.dot_general(a, b, (((1,), (1,)), ((), ())), preferred_element_type=jnp.float32)


def gelu_and_slope(x):
    c = math.sqrt(2.0 / math.pi)
    th = jnp.tanh(c * (x + 0.044715 * (x * x * x)))
    slope = 0.5 * (1.0 + th) + 0.5 * x * (1.0 - th * th) * (c * (1.0 + 3.0 * 0.044715 * (x * x)))
    return 0.5 * x * (1.0 + th), slope


def copy_kernel(start, stash_ref, *refs):
    out_ref, done = refs[-2:]
    copy = pltpu.make_async_copy(stash_ref.at[pl.ds(start, out_ref.shape[0])], out_ref, done)
    copy.start()
    copy.wait()


def rows_after(stash, start, rows, waits):
    return pl.pallas_call(
        functools.partial(copy_kernel, start),
        out_shape=jax.ShapeDtypeStruct((rows, stash.shape[1]), stash.dtype),
        in_specs=[ANY] * (1 + len(waits)),
        out_specs=VMEM,
        scratch_shapes=[pltpu.SemaphoreType.DMA],
        compiler_params=SMALL,
    )(stash, *waits)


def chunk_kernel(start, joins, waits, me_ref, saved_ref, cot_ref, dact_ref, down_ref, gain_ref, *refs):
    outs = refs[joins + waits :]
    dx_ref, pack_refs, normed_ref = outs[0], outs[1:-1], outs[-1]
    groups = len(pack_refs)
    rows, features = saved_ref.shape
    ahead = dx_ref.shape[0] - rows
    at = 0
    for part in refs[:joins]:
        dx_ref[pl.ds(at, part.shape[0]), :] = part[...]
        at += part.shape[0]
    width = features // groups
    rank = down_ref.shape[1]
    lanes = [pl.ds(f, LANES) for f in range(0, features, LANES)]
    total = jnp.zeros((rows, 1), jnp.float32)
    for at in lanes:
        xf = saved_ref[:, at].astype(jnp.float32)
        total += jnp.sum(xf * xf, axis=1, keepdims=True)
    inverse = 1.0 / jnp.sqrt(total / features + 1e-05)
    for at in lanes:
        unit = saved_ref[:, at].astype(jnp.float32) * inverse
        normed_ref[:, at] = (unit * gain_ref[:, at]).astype(jnp.bfloat16)
    pre = jnp.dot(normed_ref[...], down_ref[...], preferred_element_type=jnp.float32)
    act, slope = gelu_and_slope(pre)
    act = act.astype(jnp.bfloat16)
    dpre = (dact_ref[pl.ds(start, rows), :] * slope).astype(jnp.bfloat16)
    inner = jnp.sum(dpre.astype(jnp.float32) * pre, axis=1, keepdims=True) / features
    for k in range(groups):
        at = pl.ds(pl.multiple_of((me_ref[0] ^ k) * width, 128), width)
        pack_refs[k][:, :width] = normed_ref[:, at]
        pack_refs[k][:, width : width + rank] = dpre
        pack_refs[k][:, width + rank :] = act
    pull = inner * inverse
    for at in lanes:
        dnorm = last_dot(dpre, down_ref[at, :]) * gain_ref[:, at]
        xf = saved_ref[:, at].astype(jnp.float32)
        held = cot_ref[pl.ds(start, rows), at].astype(jnp.float32)
        dx_ref[pl.ds(ahead, rows), at] = (held + (dnorm - xf * pull) * inverse).astype(jnp.bfloat16)


def run_chunk(me, saved, cot, dact, down, gain, start, joins, waits, groups, cost):
    rows, features = saved.shape
    rank = down.shape[1]
    pack = jax.ShapeDtypeStruct((rows, features // groups + 2 * rank), jnp.bfloat16)
    ahead = sum(part.shape[0] for part in joins)
    outs = [jax.ShapeDtypeStruct((ahead + rows, features), jnp.bfloat16)] + [pack] * groups
    got = pl.pallas_call(
        functools.partial(chunk_kernel, start, len(joins), len(waits)),
        out_shape=outs,
        in_specs=[SMEM] + [VMEM] * (5 + len(joins)) + [ANY] * len(waits),
        out_specs=[VMEM] * len(outs),
        scratch_shapes=[pltpu.VMEM((rows, features), jnp.bfloat16)],
        cost_estimate=cost,
        compiler_params=PARAMS,
    )(me, saved, cot, dact, down, gain, *joins, *waits)
    return got[0], got[1:]


def gather_rows(groups, spans, packs, cots, every, held):
    at = 0
    for k in range(groups):
        for j, (start, rows) in enumerate(spans):
            every[pl.ds(at, rows), :] = packs[k * len(spans) + j][...]
            held[pl.ds(at, rows), :] = cots[k][pl.ds(start, rows), :]
            at += rows


def sum_kernel(groups, spans, *refs):
    count = groups * len(spans)
    packs, cots = refs[:count], refs[count : count + groups]
    down_ref, up_ref, every, held = refs[-4:]
    width, rank = down_ref.shape
    gather_rows(groups, spans, packs, cots, every, held)
    down_ref[...] = rows_dot(every[:, :width], every[:, width : width + rank])
    up_ref[...] = rows_dot(every[:, width + rank :], held[...])


def final_kernel(groups, spans, *refs):
    packs, cots = refs[:groups], refs[groups : 2 * groups]
    old_down, old_up, first = refs[2 * groups : 2 * groups + 3]
    before_ref, down_ref, up_ref, every, held, down, up, done = refs[2 * groups + 3 :]
    width, rank = down.shape
    copies = [
        pltpu.make_async_copy(first, before_ref.at[pl.ds(0, first.shape[0])], done.at[0]),
        pltpu.make_async_copy(down, down_ref, done.at[1]),
        pltpu.make_async_copy(up, up_ref, done.at[2]),
    ]
    copies[0].start()
    gather_rows(groups, spans, packs, cots, every, held)
    down[...] = old_down[...] + rows_dot(every[:, :width], every[:, width : width + rank])
    copies[1].start()
    up[...] = old_up[...] + rows_dot(every[:, width + rank :], held[...])
    copies[2].start()
    for copy in copies:
        copy.wait()


def join_kernel(start, before_ref, last, out_ref, done):
    copy = pltpu.make_async_copy(last, out_ref.at[pl.ds(start, last.shape[0])], done)
    copy.start()
    copy.wait()


def run_join(before, last):
    return pl.pallas_call(
        functools.partial(join_kernel, before.shape[0] - last.shape[0]),
        out_shape=jax.ShapeDtypeStruct(before.shape, before.dtype),
        in_specs=[ANY, ANY],
        out_specs=ANY,
        scratch_shapes=[pltpu.SemaphoreType.DMA],
        input_output_aliases={0: 0},
        compiler_params=SMALL,
    )(before, last)


def operands(packs, cots, spans):
    groups = len(cots)
    width = cots[0].shape[1]
    depth = groups * sum(rows for _, rows in spans)
    args = [packs[j][k] for k in range(groups) for j in range(len(spans))] + list(cots)
    scratch = [
        pltpu.VMEM((depth, packs[0][0].shape[1]), jnp.bfloat16),
        pltpu.VMEM((depth, width), jnp.bfloat16),
    ]
    return groups, width, args, scratch


def run_sum(packs, cots, spans, waits, rank):
    groups, width, args, scratch = operands(packs, cots, spans)
    return pl.pallas_call(
        functools.partial(sum_kernel, groups, spans),
        out_shape=[
            jax.ShapeDtypeStruct((width, rank), jnp.float32),
            jax.ShapeDtypeStruct((rank, width), jnp.float32),
        ],
        in_specs=[VMEM] * len(args) + [ANY] * len(waits),
        out_specs=[VMEM] * 2,
        scratch_shapes=scratch,
        compiler_params=PARAMS,
    )(*args, *waits)


def run_final(packs, cots, spans, partial, first, tokens):
    groups, width, args, scratch = operands(packs, cots, spans)
    down, up = [jax.ShapeDtypeStruct(value.shape, jnp.float32) for value in partial]
    scratch += [
        pltpu.VMEM(down.shape, jnp.float32),
        pltpu.VMEM(up.shape, jnp.float32),
        pltpu.SemaphoreType.DMA((3,)),
    ]
    return pl.pallas_call(
        functools.partial(final_kernel, groups, spans),
        out_shape=[jax.ShapeDtypeStruct((tokens, first.shape[1]), first.dtype), down, up],
        in_specs=[VMEM] * (len(args) + 3),
        out_specs=[ANY] * 3,
        scratch_shapes=scratch,
        compiler_params=PARAMS,
        cost_estimate=SUMCOST,
    )(*args, *partial, first)


def per_device(stash_held, grad_in, w_down, w_up, gain):
    sections = lax.axis_size("pipe")
    groups = lax.axis_size("dp")
    me = lax.axis_index("dp")
    stash, cot, down, upper = stash_held[0], grad_in[0], w_down[0], w_up[0]
    tokens, features = cot.shape
    rank = down.shape[1]
    width = features // groups
    sizes = [tokens * share // sum(SHARES) for share in SHARES]
    spans = [(sum(sizes[:i]), size) for i, size in enumerate(sizes)]
    chunks = len(spans)

    def held(value):
        return exchanged(value, "pipe", sections // 2)

    arrivals = [held(stash[start : start + rows]) for start, rows in spans[:2]]
    cot_all = []
    for k in range(groups):
        part = lax.dynamic_slice_in_dim(cot, (me ^ k) * width, width, axis=1)
        cot_all.append(exchanged(part, "dp", k) if k else part)
    dact = last_dot(cot, upper)
    index = jnp.reshape(me.astype(jnp.int32), (1,))

    parts, packs, waits = [], [], cot_all[1:]
    for i, (start, rows) in enumerate(spans):
        if i + 2 < chunks:
            coming = rows_after(stash, *spans[i + 2], [arrivals[i]] + waits[:1] * (i > 0))
            arrivals.append(held(coming))
            waits = waits + [coming]
        joins = parts if i == chunks - 2 else []
        dx, pack = run_chunk(index, arrivals[i], cot, dact, down, gain, start, joins, waits, groups, COSTS[i])
        packs.append([exchanged(pack[k], "dp", k) if k else pack[k] for k in range(groups)])
        parts.append(dx)
        waits = packs[-1][1:]
    first, last = [to_previous(dx, "pipe") for dx in parts[-2:]]
    partial = run_sum(packs[:-1], cot_all, spans[:-1], [pack[0]], rank)
    before, down_grad, up_grad = run_final(
        packs[-1:], cot_all, spans[-1:], partial, first, tokens
    )
    before = run_join(before, last)
    return (before[None], down_grad[None], up_grad[None])


def solution(mesh):
    in_specs = (
        P("pipe", "dp", None),
        P("pipe", "dp", None),
        P("pipe", None, None),
        P("pipe", None, None),
        P("pipe", None),
    )
    out_specs = (P("pipe", "dp", None), P("pipe", "dp", None), P("pipe", None, "dp"))
    return jax.shard_map(
        per_device, mesh=mesh, in_specs=in_specs, out_specs=out_specs, check_vma=False
    )
```
